256 devices in a mesh: row: 16 (over y, x), col: 16 (over z, core).
Axes of the slice: x: 4, y: 4, z: 8, core: 2. Of those that a mesh axis runs over, the one named last changes fastest.
Arguments:
- matrix: bfloat16 [8192, 8192], P('row', 'col'), may hold values from -0.1875 to 0.1875
- pattern: int32 [128, 128], P('row', 'col'), may hold values 0 or 1
Outputs:
- sign_step: bfloat16 [8192, 8192], P('row', 'col')
The draws below stay inside these ranges and needn't reach their ends.
All inputs are finite; a program needn't handle non-finite values. No bound on the sum of `pattern` on one device may be relied on, other than what follows from the above.
Results may differ from the reference program's by a relative error of at most 0.0042.
Values may be sent and summed in bfloat16 or wider, within the bound.
No kernel may reach another device: no remote copies, remote signals or barrier semaphores. Data moves between devices by JAX's collectives and lax.ppermute only.
A program may use at most 64 MiB of HBM per device.

```python
import jax
import jax.numpy as jnp

BLK = 64
NB = 128
NFUN = 8192


def place_ends(drawn, rng, least, top_value):
    place = [jax.random.randint(jax.random.fold_in(rng, axis), (), 0, length) for axis, length in enumerate(drawn.shape)]
    longest = drawn.shape.index(max(drawn.shape))
    next_to = place[:longest] + [(place[longest] + 1) % drawn.shape[longest]] + place[longest + 1:]
    return drawn.at[tuple(place)].set(least).at[tuple(next_to)].set(top_value)


def level_of(rng, dims, shards, low, high):
    gain, own = 1.0, jax.random.fold_in(rng, 6)
    for axis_at, blocks in shards:
        draws = jnp.exp(jax.random.uniform(jax.random.fold_in(own, axis_at), (blocks,), jnp.float32, low / len(shards), high / len(shards)))
        gain = gain * jnp.repeat(draws, dims[axis_at] // blocks).reshape([-1 if axis == axis_at else 1 for axis in range(len(dims))])
    return gain


def gaussian(own_key, extent, width, most, pieces=(), kind=jnp.bfloat16):
    drawn = jax.random.normal(own_key, extent, jnp.float32) * width
    if len(pieces) > 0:
        drawn = level_of(own_key, extent, pieces, -0.22, 0.18) * drawn
    return jnp.clip(drawn, min=-most, max=most).astype(kind)


def setup_inputs(seed: int = 0) -> dict:
    key_list = jax.random.split(jax.random.key(seed), 3)
    matrix = gaussian(key_list[0], (NFUN, NFUN), (NFUN // 8) ** -0.5, 0.1875, ((0, 16), (1, 16)))
    pattern = place_ends((jax.random.randint(key_list[1], (NB, NB), 0, 2) < 1).astype(jnp.int32), jax.random.fold_in(key_list[1], 1), 0, 1)
    return dict(matrix=matrix, pattern=pattern)


def reference(matrix, pattern):
    keep = jnp.repeat(jnp.repeat(pattern, BLK, axis=0), BLK, axis=1)
    keep_float = keep.astype(jnp.float32)
    masked = jnp.where(keep == 1, matrix, jnp.zeros_like(matrix))
    square = keep_float * jnp.dot(masked, masked, preferred_element_type=jnp.float32)
    identity = jnp.eye(NFUN, dtype=jnp.float32)
    middle = (1.5 * identity - 0.5 * square).astype(jnp.bfloat16)
    product = keep_float * jnp.dot(masked, middle, preferred_element_type=jnp.float32)
    return product.astype(jnp.bfloat16)
```

```python
import functools

import jax
import jax.numpy as jnp
from jax import lax
from jax.experimental import pallas as pl
from jax.experimental.pallas import tpu as pltpu
from jax.sharding import PartitionSpec as P

BLK = 64
SIDE = 4
CHUNKS = 2
AXES = ("row", "col")
F32 = jnp.float32
BF16 = jnp.bfloat16


def device(y, x, z, c):
    return ((y % SIDE) * SIDE + x % SIDE) * 16 + z * 2 + c


def shift_perm(dy, dx):
    return [
        (device(y, x, z, c), device(y + dy, x + dx, z, c))
        for y in range(SIDE) for x in range(SIDE) for z in range(8) for c in range(2)
    ]


def exchange_perm():
    pairs = []
    for y in range(SIDE):
        for x in range(SIDE):
            for k in range(4):
                for j in range(4):
                    pairs.append((
                        device(y, x, 2 * k + j // 2, j % 2),
                        device(y, j, 2 * k + x // 2, x % 2),
                    ))
    return pairs


def expand(pattern, rows, cols):
    br, bc = pattern.shape
    up = (lax.broadcasted_iota(jnp.int32, (rows, br), 0) // BLK
          == lax.broadcasted_iota(jnp.int32, (rows, br), 1)).astype(F32)
    across = (lax.broadcasted_iota(jnp.int32, (bc, cols), 1) // BLK
              == lax.broadcasted_iota(jnp.int32, (bc, cols), 0)).astype(F32)
    tall = jnp.dot(up, pattern.astype(F32), preferred_element_type=F32)
    return jnp.dot(tall, across, preferred_element_type=F32)


def mask_kernel(matrix_ref, pattern_ref, out_ref):
    keep = expand(pattern_ref[...], *matrix_ref.shape) == 1.0
    out_ref[...] = jnp.where(keep, matrix_ref[...], jnp.zeros_like(matrix_ref))


def mask(matrix, pattern):
    return pl.pallas_call(
        mask_kernel,
        out_shape=jax.ShapeDtypeStruct(matrix.shape, BF16),
        name="mask",
    )(matrix, pattern)


def partial_kernel(where_ref, a0, a1, a2, a3, b0, b1, b2, b3, out_ref):
    total = jnp.dot(a0[...], b0[...], preferred_element_type=F32)
    total += jnp.dot(a1[...], b1[...], preferred_element_type=F32)
    total += jnp.dot(a2[...], b2[...], preferred_element_type=F32)
    total += jnp.dot(a3[...], b3[...], preferred_element_type=F32)
    out_ref[...] = total.astype(out_ref.dtype)


def partial_product(where, held, right, step, dtype):
    size = held.shape[-1]
    cols = right[0].shape[1]
    tile = size // 2

    def held_spec(j):
        return pl.BlockSpec((None, None, tile, size), lambda i, w: (w[j], w[4 + step], i, 0))

    return pl.pallas_call(
        partial_kernel,
        grid_spec=pltpu.PrefetchScalarGridSpec(
            num_scalar_prefetch=1,
            grid=(2,),
            in_specs=[held_spec(j) for j in range(4)]
            + [pl.BlockSpec((size, cols), lambda i, w: (0, 0))] * 4,
            out_specs=pl.BlockSpec((tile, cols), lambda i, w: (i, 0)),
        ),
        out_shape=jax.ShapeDtypeStruct((size, cols), dtype),
        compiler_params=pltpu.CompilerParams(vmem_limit_bytes=24 << 20),
        cost_estimate=pl.CostEstimate(
            flops=2 * size * 4 * size * cols,
            bytes_accessed=2 * (4 * size * size + 4 * size * cols + size * cols),
            transcendentals=0),
        name="partial_product",
    )(where, held, held, held, held, *right)


def add_kernel(middle, chunk, chunks, where_ref, own, p1, p2, p3, pattern_ref, out_ref):
    rows, cols = out_ref.shape
    total = own[...] + p1[...].astype(F32) + p2[...].astype(F32) + p3[...].astype(F32)
    keep = expand(pattern_ref[...], rows, cols * chunks)[:, chunk * cols:(chunk + 1) * cols]
    total = keep * total
    if middle:
        diagonal = (lax.broadcasted_iota(jnp.int32, (rows, cols), 0) + where_ref[8]
                    == lax.broadcasted_iota(jnp.int32, (rows, cols), 1) + chunk * cols)
        total = jnp.where(diagonal, 1.5, 0.0) - 0.5 * total
    out_ref[...] = total.astype(out_ref.dtype)


def add_partials(where, parts, pattern, middle, chunk, chunks):
    rows, cols = parts[0].shape
    vmem = pl.BlockSpec(memory_space=pltpu.VMEM)
    return pl.pallas_call(
        functools.partial(add_kernel, middle, chunk, chunks),
        in_specs=[pl.BlockSpec(memory_space=pltpu.SMEM)] + [vmem] * 5,
        out_specs=vmem,
        out_shape=jax.ShapeDtypeStruct((rows, cols), BF16),
        cost_estimate=pl.CostEstimate(flops=8 * rows * cols, bytes_accessed=12 * rows * cols, transcendentals=0),
        name="add_partials",
    )(where, *parts, pattern)


def local(matrix, pattern):
    size = matrix.shape[0]
    cols = matrix.shape[1] // CHUNKS
    row, col = lax.axis_index("row"), lax.axis_index("col")
    y, x = row // SIDE, row % SIDE
    where = jnp.stack(
        [(y + SIDE - j) % SIDE for j in range(4)]
        + [(x + j) % SIDE for j in range(4)]
        + [(row - col) * size]
    ).astype(jnp.int32)

    def gather_y(block):
        return [block] + [lax.ppermute(block, AXES, shift_perm(j, 0)) for j in (1, 2, 3)]

    def reduce_x(held, right):
        sent = {}
        for step in (2, 1, 3):
            part = partial_product(where, held, right, step, BF16)
            sent[step] = lax.ppermute(part, AXES, shift_perm(0, step))
        own = partial_product(where, held, right, 0, F32)
        return [own, sent[1], sent[2], sent[3]]

    masked = mask(matrix, pattern)
    placed = lax.ppermute(masked, AXES, exchange_perm())
    held = lax.all_gather(placed, "col", axis=0, tiled=False).reshape(4, 4, size, size)
    chunks = [masked[:, k * cols:(k + 1) * cols] for k in range(CHUNKS)]
    rights = [gather_y(block) for block in chunks]
    squares = [reduce_x(held, right) for right in rights]
    middles = [add_partials(where, parts, pattern, True, k, CHUNKS) for k, parts in enumerate(squares)]
    rights = [gather_y(block) for block in middles]
    products = [reduce_x(held, right) for right in rights]
    outs = [add_partials(where, parts, pattern, False, k, CHUNKS) for k, parts in enumerate(products)]
    return jnp.concatenate(outs, axis=1)


def solution(mesh):
    spec = P("row", "col")
    return jax.shard_map(local, mesh=mesh, in_specs=(spec, spec), out_specs=spec, check_vma=False)
```

```python
import functools

import jax
import jax.numpy as jnp
from jax import lax
from jax.experimental import pallas as pl
from jax.experimental.pallas import tpu as pltpu
from jax.sharding import PartitionSpec as P

BLK = 64
SIDE = 4
DEEP = 8
PIECES = 2
CHUNKS = 2
AXES = ("row", "col")
F32 = jnp.float32
BF16 = jnp.bfloat16
VMEM = pl.BlockSpec(memory_space=pltpu.VMEM)
SMEM = pl.BlockSpec(memory_space=pltpu.SMEM)
LIMIT = pltpu.CompilerParams(vmem_limit_bytes=40 << 20)


def device(y, x, z, c):
    return ((y % SIDE) * SIDE + x % SIDE) * 2 * DEEP + (z % DEEP) * 2 + c


PLACES = [(y, x, z, c) for y in range(SIDE) for x in range(SIDE) for z in range(DEEP) for c in range(2)]


def shift_perm(dy, dx):
    return [(device(y, x, z, c), device(y + dy, x + dx, z, c)) for y, x, z, c in PLACES]


SWAP = [(device(y, x, z, c), device(y, x, z, 1 - c)) for y, x, z, c in PLACES]
RING = [(device(y, x, z, c), device(y, x, z + 1 - 2 * c, c)) for y, x, z, c in PLACES]
EXCHANGE = [
    (device(y, x, z, c), device(y, 2 * (z % 2) + c, z - z % 2 + x // 2, x % 2)) for y, x, z, c in PLACES
]


def send(block, pairs):
    return lax.ppermute(block, AXES, pairs)


def mask_kernel(matrix_ref, pattern_ref, out_ref, keep_ref):
    rows, cols = matrix_ref.shape
    br, bc = pattern_ref.shape
    up = (lax.broadcasted_iota(jnp.int32, (rows, br), 0) // BLK
          == lax.broadcasted_iota(jnp.int32, (rows, br), 1)).astype(F32).astype(BF16)
    across = (lax.broadcasted_iota(jnp.int32, (bc, cols), 1) // BLK
              == lax.broadcasted_iota(jnp.int32, (bc, cols), 0)).astype(F32).astype(BF16)
    pattern = pattern_ref[...].astype(F32).astype(BF16)
    tall = jnp.dot(up, pattern, preferred_element_type=F32).astype(BF16)
    keep = jnp.dot(tall, across, preferred_element_type=F32)
    keep_ref[...] = keep.astype(BF16)
    out_ref[...] = jnp.where(keep == 1.0, matrix_ref[...].astype(F32), 0.0).astype(BF16)


def mask(matrix, pattern):
    shape = jax.ShapeDtypeStruct(matrix.shape, BF16)
    return pl.pallas_call(
        mask_kernel, in_specs=[VMEM, VMEM], out_specs=[VMEM, VMEM], out_shape=[shape, shape], name="mask",
    )(matrix, pattern)


EVEN_OWN = [(0, 0), (2, 0), (6, 1), (4, None)]
EVEN_OTHER = [(0, 1), (2, 1), (6, 0), (8, None)]
ODD_OWN = [(1, 0), (3, 0), (5, 1), (7, 1)]
ODD_OTHER = [(1, 1), (3, 1), (5, 0), (7, 0)]
TERMS = (EVEN_OWN, EVEN_OTHER, ODD_OWN, ODD_OTHER)


def partial_kernel(first, cols, where_ref, *refs):
    held = [refs[9 * p:9 * p + 9] for p in range(PIECES)]
    right = refs[9 * PIECES:9 * PIECES + 4]
    outs = refs[9 * PIECES + 4:9 * PIECES + 8]
    stack = refs[-1]
    tall = held[0][4].shape[0]
    for j in range(4):
        stack[j] = right[j][:, first:first + cols]
    for t, terms in enumerate(TERMS):
        for p in range(PIECES):
            total = None
            for slot, which in terms:
                ref = held[p][slot]
                left = ref[...] if which is None else ref[which]
                term = jnp.dot(left, stack[where_ref[4 + slot]], preferred_element_type=F32)
                total = term if total is None else total + term
            for d in range(4):
                @pl.when(where_ref[t] == d)
                def _():
                    outs[d][p * tall:(p + 1) * tall, :] = total.astype(outs[d].dtype)


def partial_products(where, held, right, first, cols):
    tall, deep = held[0][4].shape
    rows = tall * PIECES
    return pl.pallas_call(
        functools.partial(partial_kernel, first, cols),
        in_specs=[SMEM] + [VMEM] * (9 * PIECES + 4),
        out_specs=[VMEM] * 4,
        out_shape=[jax.ShapeDtypeStruct((rows, cols), F32 if d == 0 else BF16) for d in range(4)],
        scratch_shapes=[pltpu.VMEM((4, deep, cols), BF16)],
        compiler_params=LIMIT,
        cost_estimate=pl.CostEstimate(
            flops=2 * 4 * rows * 4 * deep * cols, bytes_accessed=2 * 16 * rows * deep, transcendentals=0),
        name="partial_products",
    )(where, *[a for piece in held for a in piece], *right)


def middle_kernel(first, where_ref, own, p1, p2, p3, keep_ref, out_ref):
    rows, cols = out_ref.shape
    total = own[...] + p1[...].astype(F32) + p2[...].astype(F32) + p3[...].astype(F32)
    total = keep_ref[:, first:first + cols].astype(F32) * total
    diagonal = (lax.broadcasted_iota(jnp.int32, (rows, cols), 0) + where_ref[13]
                == lax.broadcasted_iota(jnp.int32, (rows, cols), 1) + first)
    out_ref[...] = (jnp.where(diagonal, 1.5, 0.0) - 0.5 * total).astype(BF16)


def middle(where, parts, keep, first):
    rows, cols = parts[0].shape
    return pl.pallas_call(
        functools.partial(middle_kernel, first),
        in_specs=[SMEM] + [VMEM] * 5,
        out_specs=VMEM,
        out_shape=jax.ShapeDtypeStruct((rows, cols), BF16),
        cost_estimate=pl.CostEstimate(flops=8 * rows * cols, bytes_accessed=12 * rows * cols, transcendentals=0),
        name="middle",
    )(where, *parts, keep)


def finish_kernel(*refs):
    keep_ref, out_ref = refs[-2], refs[-1]
    cols = out_ref.shape[1] // CHUNKS
    for k in range(CHUNKS):
        own, p1, p2, p3 = refs[4 * k:4 * k + 4]
        total = own[...] + p1[...].astype(F32) + p2[...].astype(F32) + p3[...].astype(F32)
        at = slice(k * cols, (k + 1) * cols)
        out_ref[:, at] = (keep_ref[:, at].astype(F32) * total).astype(BF16)


def finish(parts, keep):
    return pl.pallas_call(
        finish_kernel,
        in_specs=[VMEM] * (4 * CHUNKS + 1),
        out_specs=VMEM,
        out_shape=jax.ShapeDtypeStruct(keep.shape, BF16),
        cost_estimate=pl.CostEstimate(flops=4 * keep.size, bytes_accessed=14 * keep.size, transcendentals=0),
        name="finish",
    )(*[a for part in parts for a in part], keep)


def local(matrix, pattern):
    size = matrix.shape[0]
    tall, cols = size // PIECES, matrix.shape[1] // CHUNKS
    row, col = lax.axis_index("row"), lax.axis_index("col")
    y, x, z, c = row >> 2, row & 3, col >> 1, col & 1
    up = 2 * c - 1
    steps = [2 * (z & 1) + c, 2 * (z & 1) + 1 - c, 2 * ((z + 1) & 1) + c, 2 * ((z + 1) & 1) + 1 - c]
    chips = [z + s * up for s in range(5)] + [z - s * up for s in range(1, 5)]
    where = jnp.stack(
        [(step - x) & 3 for step in steps]
        + [(y - ((chip & 7) >> 1)) & 3 for chip in chips]
        + [(row - col) * size]
    ).astype(jnp.int32)

    def gather_y(block):
        return [block] + [send(block, shift_perm(j, 0)) for j in (1, 2, 3)]

    def reduce_x(right, first):
        own, *parts = partial_products(where, held, right, first, cols)
        sent = {d: send(parts[d - 1], shift_perm(0, d)) for d in (2, 1, 3)}
        return [own, sent[1], sent[2], sent[3]]

    masked, keep = mask(matrix, pattern)
    held = []
    for p in range(PIECES):
        placed = send(masked[p * tall:(p + 1) * tall], EXCHANGE)
        own = jnp.stack([placed, send(placed, SWAP)])
        r1 = send(own, RING)
        r2 = send(r1, RING)
        r3 = send(r2, RING)
        r4 = send(r3[0], RING)
        held.append([own, r1, r2, r3, r4] + [send(r, SWAP) for r in (r1, r2, r3, r4)])
    right = gather_y(masked)
    squares = [reduce_x(right, k * cols) for k in range(CHUNKS)]
    middles = [middle(where, parts, keep, k * cols) for k, parts in enumerate(squares)]
    products = [reduce_x(gather_y(block), 0) for block in middles]
    return finish(products, keep)


def solution(mesh):
    spec = P("row", "col")
    return jax.shard_map(local, mesh=mesh, in_specs=(spec, spec), out_specs=spec, check_vma=False)
```

```python
import functools

import jax
import jax.numpy as jnp
from jax import lax
from jax.experimental import pallas as pl
from jax.experimental.pallas import tpu as pltpu
from jax.sharding import PartitionSpec as P

BLK = 64
SIDE = 4
DEEP = 8
PIECES = 2
CHUNKS = 2
AXES = ("row", "col")
F32 = jnp.float32
BF16 = jnp.bfloat16
VMEM = pl.BlockSpec(memory_space=pltpu.VMEM)
SMEM = pl.BlockSpec(memory_space=pltpu.SMEM)
SMALL = pltpu.CompilerParams(vmem_limit_bytes=4 << 20)
LARGE = pltpu.CompilerParams(vmem_limit_bytes=16 << 20)
Y_GROUPS = [[y * SIDE + x for y in range(SIDE)] for x in range(SIDE)]


def device(y, x, z, c):
    return ((y % SIDE) * SIDE + x % SIDE) * 2 * DEEP + (z % DEEP) * 2 + c


PLACES = [(y, x, z, c) for y in range(SIDE) for x in range(SIDE) for z in range(DEEP) for c in range(2)]


def shift_perm(dy, dx):
    return [(device(y, x, z, c), device(y + dy, x + dx, z, c)) for y, x, z, c in PLACES]


SWAP = [(device(y, x, z, c), device(y, x, z, 1 - c)) for y, x, z, c in PLACES]
RING = [(device(y, x, z, c), device(y, x, z + 1 - 2 * c, c)) for y, x, z, c in PLACES]
EXCHANGE = [
    (device(y, x, z, c), device(y, 2 * (z % 2) + c, z - z % 2 + x // 2, x % 2)) for y, x, z, c in PLACES
]


def send(block, pairs):
    return lax.ppermute(block, AXES, pairs)


def mask_kernel(matrix_ref, pattern_ref, out_ref, keep_ref):
    rows, cols = matrix_ref.shape
    br, bc = pattern_ref.shape
    up = (lax.broadcasted_iota(jnp.int32, (rows, br), 0) // BLK
          == lax.broadcasted_iota(jnp.int32, (rows, br), 1)).astype(F32).astype(BF16)
    across = (lax.broadcasted_iota(jnp.int32, (bc, cols), 1) // BLK
              == lax.broadcasted_iota(jnp.int32, (bc, cols), 0)).astype(F32).astype(BF16)
    pattern = pattern_ref[...].astype(F32).astype(BF16)
    tall = jnp.dot(up, pattern, preferred_element_type=F32).astype(BF16)
    keep = jnp.dot(tall, across, preferred_element_type=F32)
    keep_ref[...] = keep.astype(BF16)
    out_ref[...] = jnp.where(keep == 1.0, matrix_ref[...].astype(F32), 0.0).astype(BF16)


def mask(matrix, pattern):
    shape = jax.ShapeDtypeStruct(matrix.shape, BF16)
    return pl.pallas_call(
        mask_kernel, in_specs=[VMEM, VMEM], out_specs=[VMEM, VMEM], out_shape=[shape, shape],
        compiler_params=SMALL, name="mask",
    )(matrix, pattern)


EVEN_OWN = [(0, 0), (2, 0), (6, 1), (4, None)]
EVEN_OTHER = [(0, 1), (2, 1), (6, 0), (8, None)]
ODD_OWN = [(1, 0), (3, 0), (5, 1), (7, 1)]
ODD_OTHER = [(1, 1), (3, 1), (5, 0), (7, 0)]
TERMS = (EVEN_OWN, EVEN_OTHER, ODD_OWN, ODD_OTHER)


def partial_kernel(first, cols, where_ref, *refs):
    held = [refs[9 * p:9 * p + 9] for p in range(PIECES)]
    right = refs[9 * PIECES:-5]
    outs = refs[-5:-1]
    stack = refs[-1]
    tall = held[0][4].shape[0]
    base = 14 if len(right) == 1 else 4
    for j in range(4):
        stack[j] = right[0][j, :, first:first + cols] if len(right) == 1 else right[j][:, first:first + cols]
    for t, terms in enumerate(TERMS):
        for p in range(PIECES):
            total = None
            for slot, which in terms:
                ref = held[p][slot]
                left = ref[...] if which is None else ref[which]
                term = jnp.dot(left, stack[where_ref[base + slot]], preferred_element_type=F32)
                total = term if total is None else total + term
            for d in range(4):
                @pl.when(where_ref[t] == d)
                def _():
                    outs[d][p * tall:(p + 1) * tall, :] = total.astype(outs[d].dtype)


def partial_products(where, held, right, first, cols):
    tall, deep = held[0][4].shape
    rows = tall * PIECES
    return pl.pallas_call(
        functools.partial(partial_kernel, first, cols),
        in_specs=[SMEM] + [VMEM] * (9 * PIECES + len(right)),
        out_specs=[VMEM] * 4,
        out_shape=[jax.ShapeDtypeStruct((rows, cols), F32 if d == 0 else BF16) for d in range(4)],
        scratch_shapes=[pltpu.VMEM((4, deep, cols), BF16)],
        compiler_params=LARGE,
        cost_estimate=pl.CostEstimate(
            flops=2 * 4 * rows * 4 * deep * cols, bytes_accessed=2 * 16 * rows * deep, transcendentals=0),
        name="partial_products",
    )(where, *[a for piece in held for a in piece], *right)


def middle_kernel(first, where_ref, own, p1, p2, p3, keep_ref, out_ref):
    rows, cols = out_ref.shape
    total = own[...] + p1[...].astype(F32) + p2[...].astype(F32) + p3[...].astype(F32)
    total = keep_ref[:, first:first + cols].astype(F32) * total
    diagonal = (lax.broadcasted_iota(jnp.int32, (rows, cols), 0) + where_ref[13]
                == lax.broadcasted_iota(jnp.int32, (rows, cols), 1) + first)
    out_ref[...] = (jnp.where(diagonal, 1.5, 0.0) - 0.5 * total).astype(BF16)


def middle(where, parts, keep, first):
    rows, cols = parts[0].shape
    return pl.pallas_call(
        functools.partial(middle_kernel, first),
        in_specs=[SMEM] + [VMEM] * 5,
        out_specs=VMEM,
        out_shape=jax.ShapeDtypeStruct((rows, cols), BF16),
        cost_estimate=pl.CostEstimate(flops=8 * rows * cols, bytes_accessed=12 * rows * cols, transcendentals=0),
        compiler_params=SMALL,
        name="middle",
    )(where, *parts, keep)


def finish_kernel(*refs):
    keep_ref, out_ref = refs[-2], refs[-1]
    cols = out_ref.shape[1] // CHUNKS
    for k in range(CHUNKS):
        own, p1, p2, p3 = refs[4 * k:4 * k + 4]
        total = own[...] + p1[...].astype(F32) + p2[...].astype(F32) + p3[...].astype(F32)
        at = slice(k * cols, (k + 1) * cols)
        out_ref[:, at] = (keep_ref[:, at].astype(F32) * total).astype(BF16)


def finish(parts, keep):
    return pl.pallas_call(
        finish_kernel,
        in_specs=[VMEM] * (4 * CHUNKS + 1),
        out_specs=VMEM,
        out_shape=jax.ShapeDtypeStruct(keep.shape, BF16),
        cost_estimate=pl.CostEstimate(flops=4 * keep.size, bytes_accessed=14 * keep.size, transcendentals=0),
        compiler_params=SMALL,
        name="finish",
    )(*[a for part in parts for a in part], keep)


def local(matrix, pattern):
    size = matrix.shape[0]
    tall, cols = size // PIECES, matrix.shape[1] // CHUNKS
    row, col = lax.axis_index("row"), lax.axis_index("col")
    y, x, z, c = row >> 2, row & 3, col >> 1, col & 1
    up = 2 * c - 1
    steps = [2 * (z & 1) + c, 2 * (z & 1) + 1 - c, 2 * ((z + 1) & 1) + c, 2 * ((z + 1) & 1) + 1 - c]
    chips = [z + s * up for s in range(5)] + [z - s * up for s in range(1, 5)]
    where = jnp.stack(
        [(step - x) & 3 for step in steps]
        + [(y - ((chip & 7) >> 1)) & 3 for chip in chips]
        + [(row - col) * size]
        + [(chip & 7) >> 1 for chip in chips]
    ).astype(jnp.int32)

    def gather_y(block):
        return [block] + [send(block, shift_perm(j, 0)) for j in (1, 2, 3)]

    def reduce_x(right, first):
        own, *parts = partial_products(where, held, right, first, cols)
        sent = {d: send(parts[d - 1], shift_perm(0, d)) for d in (2, 1, 3)}
        return [own, sent[1], sent[2], sent[3]]

    masked, keep = mask(matrix, pattern)
    held = []
    for p in range(PIECES):
        placed = send(masked[p * tall:(p + 1) * tall], EXCHANGE)
        own = jnp.stack([placed, send(placed, SWAP)])
        r1 = send(own, RING)
        r2 = send(r1, RING)
        r3 = send(r2, RING)
        r4 = send(r3[0], RING)
        held.append([own, r1, r2, r3, r4] + [send(r, SWAP) for r in (r1, r2, r3, r4)])
    right = [lax.all_gather(masked, "row", axis_index_groups=Y_GROUPS, axis=0, tiled=False)]
    squares = [reduce_x(right, k * cols) for k in range(CHUNKS)]
    middles = [middle(where, parts, keep, k * cols) for k, parts in enumerate(squares)]
    products = [reduce_x(gather_y(block), 0) for block in middles]
    return finish(products, keep)


def solution(mesh):
    spec = P("row", "col")
    return jax.shard_map(local, mesh=mesh, in_specs=(spec, spec), out_specs=spec, check_vma=False)
```

```python
import functools

import jax
import jax.numpy as jnp
from jax import lax
from jax.experimental import pallas as pl
from jax.experimental.pallas import tpu as pltpu
from jax.sharding import PartitionSpec as P

BLK = 64
SIDE = 4
DEEP = 8
PIECES = (512,)
CHUNKS = 2
AXES = ("row", "col")
F32 = jnp.float32
BF16 = jnp.bfloat16
VMEM = pl.BlockSpec(memory_space=pltpu.VMEM)
SMEM = pl.BlockSpec(memory_space=pltpu.SMEM)
SMALL = pltpu.CompilerParams(vmem_limit_bytes=4 << 20)
LARGE = pltpu.CompilerParams(vmem_limit_bytes=16 << 20)


def device(y, x, z, c):
    return ((y % SIDE) * SIDE + x % SIDE) * 2 * DEEP + (z % DEEP) * 2 + c


PLACES = [(y, x, z, c) for y in range(SIDE) for x in range(SIDE) for z in range(DEEP) for c in range(2)]


def shift_perm(dy, dx):
    return [(device(y, x, z, c), device(y + dy, x + dx, z, c)) for y, x, z, c in PLACES]


SWAP = [(device(y, x, z, c), device(y, x, z, 1 - c)) for y, x, z, c in PLACES]
RING = [(device(y, x, z, c), device(y, x, z + 1 - 2 * c, c)) for y, x, z, c in PLACES]
EXCHANGE = [
    (device(y, x, z, c), device(y, 2 * (z % 2) + c, z - z % 2 + x // 2, x % 2)) for y, x, z, c in PLACES
]


def send(block, pairs):
    return lax.ppermute(block, AXES, pairs)


def mask_kernel(matrix_ref, pattern_ref, out_ref, keep_ref):
    rows, cols = matrix_ref.shape
    br, bc = pattern_ref.shape
    up = (lax.broadcasted_iota(jnp.int32, (rows, br), 0) // BLK
          == lax.broadcasted_iota(jnp.int32, (rows, br), 1)).astype(F32).astype(BF16)
    across = (lax.broadcasted_iota(jnp.int32, (bc, cols), 1) // BLK
              == lax.broadcasted_iota(jnp.int32, (bc, cols), 0)).astype(F32).astype(BF16)
    pattern = pattern_ref[...].astype(F32).astype(BF16)
    tall = jnp.dot(up, pattern, preferred_element_type=F32).astype(BF16)
    keep = jnp.dot(tall, across, preferred_element_type=F32)
    keep_ref[...] = keep.astype(BF16)
    out_ref[...] = jnp.where(keep == 1.0, matrix_ref[...].astype(F32), 0.0).astype(BF16)


def mask(matrix, pattern):
    shape = jax.ShapeDtypeStruct(matrix.shape, BF16)
    return pl.pallas_call(
        mask_kernel, in_specs=[VMEM, VMEM], out_specs=[VMEM, VMEM], out_shape=[shape, shape],
        compiler_params=SMALL, name="mask",
    )(matrix, pattern)


EVEN_OWN = [(0, 0), (2, 2), (4, 4), (14, 6)]
EVEN_OTHER = [(5, 0), (7, 2), (10, 6), (12, 4)]
ODD_OWN = [(1, 1), (3, 3), (13, 5), (15, 7)]
ODD_OTHER = [(6, 1), (8, 3), (9, 5), (11, 7)]
TERMS = (EVEN_OWN, EVEN_OTHER, ODD_OWN, ODD_OTHER)
TILES = 16


def partial_kernel(first, cols, where_ref, *refs):
    count = len(PIECES)
    held = [refs[TILES * p:TILES * p + TILES] for p in range(count)]
    right = refs[TILES * count:-6]
    outs = refs[-6:-2]
    stack, sums = refs[-2:]
    for j in range(4):
        stack[j] = right[j][:, first:first + cols]
    for t, terms in enumerate(TERMS):
        start = 0
        for p in range(count):
            total = None
            for tile, place in terms:
                term = jnp.dot(held[p][tile][...], stack[where_ref[4 + place]], preferred_element_type=F32)
                total = term if total is None else total + term
            sums[where_ref[t], start:start + PIECES[p], :] = total
            start += PIECES[p]
    for d in range(4):
        outs[d][...] = sums[d].astype(outs[d].dtype)


def partial_products(where, held, right, first, cols):
    rows, deep = sum(PIECES), held[0][0].shape[1]
    return pl.pallas_call(
        functools.partial(partial_kernel, first, cols),
        in_specs=[SMEM] + [VMEM] * (TILES * len(PIECES) + len(right)),
        out_specs=[VMEM] * 4,
        out_shape=[jax.ShapeDtypeStruct((rows, cols), F32 if d == 0 else BF16) for d in range(4)],
        scratch_shapes=[pltpu.VMEM((4, deep, cols), BF16), pltpu.VMEM((4, rows, cols), F32)],
        compiler_params=LARGE,
        cost_estimate=pl.CostEstimate(
            flops=2 * 4 * rows * 4 * deep * cols, bytes_accessed=2 * 16 * rows * deep, transcendentals=0),
        name="partial_products",
    )(where, *[a for piece in held for a in piece], *right)


def middle_kernel(first, where_ref, own, p1, p2, p3, keep_ref, out_ref):
    rows, cols = out_ref.shape
    total = own[...] + p1[...].astype(F32) + p2[...].astype(F32) + p3[...].astype(F32)
    total = keep_ref[:, first:first + cols].astype(F32) * total
    diagonal = (lax.broadcasted_iota(jnp.int32, (rows, cols), 0) + where_ref[12]
                == lax.broadcasted_iota(jnp.int32, (rows, cols), 1) + first)
    out_ref[...] = (jnp.where(diagonal, 1.5, 0.0) - 0.5 * total).astype(BF16)


def middle(where, parts, keep, first):
    rows, cols = parts[0].shape
    return pl.pallas_call(
        functools.partial(middle_kernel, first),
        in_specs=[SMEM] + [VMEM] * 5,
        out_specs=VMEM,
        out_shape=jax.ShapeDtypeStruct((rows, cols), BF16),
        cost_estimate=pl.CostEstimate(flops=8 * rows * cols, bytes_accessed=12 * rows * cols, transcendentals=0),
        compiler_params=SMALL,
        name="middle",
    )(where, *parts, keep)


def finish_kernel(*refs):
    keep_ref, out_ref = refs[-2], refs[-1]
    cols = out_ref.shape[1] // CHUNKS
    for k in range(CHUNKS):
        own, p1, p2, p3 = refs[4 * k:4 * k + 4]
        total = own[...] + p1[...].astype(F32) + p2[...].astype(F32) + p3[...].astype(F32)
        at = slice(k * cols, (k + 1) * cols)
        out_ref[:, at] = (keep_ref[:, at].astype(F32) * total).astype(BF16)


def finish(parts, keep):
    return pl.pallas_call(
        finish_kernel,
        in_specs=[VMEM] * (4 * CHUNKS + 1),
        out_specs=VMEM,
        out_shape=jax.ShapeDtypeStruct(keep.shape, BF16),
        cost_estimate=pl.CostEstimate(flops=4 * keep.size, bytes_accessed=14 * keep.size, transcendentals=0),
        compiler_params=SMALL,
        name="finish",
    )(*[a for part in parts for a in part], keep)


def local(matrix, pattern):
    size = matrix.shape[0]
    cols = matrix.shape[1] // CHUNKS
    row, col = lax.axis_index("row"), lax.axis_index("col")
    y, x, z, c = row >> 2, row & 3, col >> 1, col & 1
    up = 1 - 2 * c
    steps = [2 * (z & 1) + c, 2 * (z & 1) + 1 - c, 2 * ((z + 1) & 1) + c, 2 * ((z + 1) & 1) + 1 - c]
    chips = [z - s * up for s in range(5)] + [z + s * up for s in range(1, 4)]
    where = jnp.stack(
        [(step - x) & 3 for step in steps]
        + [(y - ((chip & 7) >> 1)) & 3 for chip in chips]
        + [(row - col) * size]
    ).astype(jnp.int32)

    def gather_y(block):
        return [block] + [send(block, shift_perm(j, 0)) for j in (1, 2, 3)]

    def reduce_x(right, first):
        own, *parts = partial_products(where, held, right, first, cols)
        sent = {d: send(parts[d - 1], shift_perm(0, d)) for d in (2, 1, 3)}
        return [own, sent[1], sent[2], sent[3]]

    matrix, where = lax.optimization_barrier((matrix, where))
    masked, keep = mask(matrix, pattern)
    held = []
    pieces, first = [], 0
    for rows in PIECES:
        pieces.append(masked[first:first + rows])
        first += rows
    placed = [send(piece, EXCHANGE) for piece in pieces]
    y1, y3 = send(masked, shift_perm(1, 0)), send(masked, shift_perm(3, 0))
    y1, y3, masked, *placed = lax.optimization_barrier((y1, y3, masked, *placed))
    y2 = send(masked, shift_perm(2, 0))
    right = [masked, y1, y2, y3]
    for piece in placed:
        own = [piece]
        other = [send(own[0], SWAP)]
        for _ in range(4):
            own.append(send(own[-1], RING))
        for _ in range(3):
            other.append(send(other[-1], RING))
        held.append(own + other + [send(a, SWAP) for a in own[1:]] + [send(a, SWAP) for a in other[1:]])
    squares = [reduce_x(right, k * cols) for k in range(CHUNKS)]
    middles = [middle(where, parts, keep, k * cols) for k, parts in enumerate(squares)]
    products = [reduce_x(gather_y(block), 0) for block in middles]
    return finish(products, keep)


def solution(mesh):
    spec = P("row", "col")
    return jax.shard_map(local, mesh=mesh, in_specs=(spec, spec), out_specs=spec, check_vma=False)
```

```python
import functools

import jax
import jax.numpy as jnp
from jax import lax
from jax.experimental import pallas as pl
from jax.experimental.pallas import tpu as pltpu
from jax.sharding import PartitionSpec as P

BLK = 64
SIDE = 4
DEEP = 8
TILES = 16
AXES = ("row", "col")
F32 = jnp.float32
BF16 = jnp.bfloat16
VMEM = pl.BlockSpec(memory_space=pltpu.VMEM)
SMEM = pl.BlockSpec(memory_space=pltpu.SMEM)
SMALL = pltpu.CompilerParams(vmem_limit_bytes=4 << 20)
LARGE = pltpu.CompilerParams(vmem_limit_bytes=16 << 20)


def device(y, x, z, c):
    return ((y % SIDE) * SIDE + x % SIDE) * 2 * DEEP + (z % DEEP) * 2 + c


PLACES = [(y, x, z, c) for y in range(SIDE) for x in range(SIDE) for z in range(DEEP) for c in range(2)]
SWAP = [(device(y, x, z, c), device(y, x, z, 1 - c)) for y, x, z, c in PLACES]
RING = [(device(y, x, z, c), device(y, x, z + 1 - 2 * c, c)) for y, x, z, c in PLACES]


def first_axis(step):
    return [(device(y, x, z, c), device(y + step * c, x + step * (1 - c), z, c)) for y, x, z, c in PLACES]


def second_axis(step):
    return [(device(y, x, z, c), device(y + step * (1 - c), x + step * c, z, c)) for y, x, z, c in PLACES]


def send(block, pairs):
    return lax.ppermute(block, AXES, pairs)


def mask_kernel(matrix_ref, pattern_ref, out_ref, keep_ref):
    rows, cols = matrix_ref.shape
    br, bc = pattern_ref.shape
    up = (lax.broadcasted_iota(jnp.int32, (rows, br), 0) // BLK
          == lax.broadcasted_iota(jnp.int32, (rows, br), 1)).astype(F32).astype(BF16)
    across = (lax.broadcasted_iota(jnp.int32, (bc, cols), 1) // BLK
              == lax.broadcasted_iota(jnp.int32, (bc, cols), 0)).astype(F32).astype(BF16)
    pattern = pattern_ref[...].astype(F32).astype(BF16)
    tall = jnp.dot(up, pattern, preferred_element_type=F32).astype(BF16)
    keep = jnp.dot(tall, across, preferred_element_type=F32)
    keep_ref[...] = keep.astype(BF16)
    out_ref[...] = jnp.where(keep == 1.0, matrix_ref[...].astype(F32), 0.0).astype(BF16)


def mask(matrix, pattern):
    shape = jax.ShapeDtypeStruct(matrix.shape, BF16)
    return pl.pallas_call(
        mask_kernel, in_specs=[VMEM, VMEM], out_specs=[VMEM, VMEM], out_shape=[shape, shape],
        compiler_params=SMALL, name="mask",
    )(matrix, pattern)


def join_kernel(*refs):
    out_ref, first = refs[-1], 0
    for ref in refs[:-1]:
        out_ref[first:first + ref.shape[0], :] = ref[...]
        first += ref.shape[0]


def join(*parts):
    rows, cols = sum(part.shape[0] for part in parts), parts[0].shape[1]
    return pl.pallas_call(
        join_kernel, in_specs=[VMEM] * len(parts), out_specs=VMEM,
        out_shape=jax.ShapeDtypeStruct((rows, cols), BF16),
        compiler_params=SMALL, name="join",
    )(*parts)


def arrange_kernel(where_ref, *refs):
    tiles, out_ref = refs[:-1], refs[-1]
    cols = tiles[0].shape[1]
    for t, tile in enumerate(tiles):
        at = pl.multiple_of(where_ref[TILES + t] * cols, cols)
        out_ref[where_ref[t], :, pl.ds(at, cols)] = tile[...]


def arrange(where, tiles):
    rows, cols = tiles[0].shape
    return pl.pallas_call(
        arrange_kernel, in_specs=[SMEM] + [VMEM] * TILES, out_specs=VMEM,
        out_shape=jax.ShapeDtypeStruct((TILES // 2, rows, 2 * cols), BF16),
        compiler_params=SMALL, name="arrange",
    )(where, *tiles)


def cost(pairs, panel, right):
    rows, deep, cols = panel.shape[1], right.shape[0], right.shape[1]
    return pl.CostEstimate(
        flops=2 * pairs * rows * deep * cols, bytes_accessed=2 * pairs * deep * (rows + cols), transcendentals=0)


def total_of(panel_ref, rights, places):
    total = None
    for ref, (pair, first) in zip(rights, places):
        width = panel_ref.shape[2]
        for top in range(0, ref.shape[0], width):
            rows = min(width, ref.shape[0] - top)
            left = panel_ref[pair + top // width, :, first:first + rows]
            term = jnp.dot(left, ref[top:top + rows, :], preferred_element_type=F32)
            total = term if total is None else total + term
    return total


def begin_kernel(places, panel_ref, *refs):
    refs[-1][...] = total_of(panel_ref, refs[:-1], places)


def begin(panel, rights, places):
    return pl.pallas_call(
        functools.partial(begin_kernel, places), in_specs=[VMEM] * (1 + len(rights)), out_specs=VMEM,
        out_shape=jax.ShapeDtypeStruct((panel.shape[1], rights[0].shape[1]), F32),
        compiler_params=LARGE, cost_estimate=cost(6, panel, rights[0]), name="begin",
    )(panel, *rights)


def finish_kernel(middle, places, where_ref, panel_ref, sum_ref, *refs):
    keep_ref, out_ref = refs[-2:]
    total = sum_ref[...] + total_of(panel_ref, refs[:-2], places)
    total = keep_ref[...].astype(F32) * total
    if middle:
        diagonal = (lax.broadcasted_iota(jnp.int32, total.shape, 0) + where_ref[2 * TILES]
                    == lax.broadcasted_iota(jnp.int32, total.shape, 1))
        total = jnp.where(diagonal, 1.5, 0.0) - 0.5 * total
    out_ref[...] = total.astype(BF16)


def finish(where, panel, begun, rights, places, keep, middle):
    return pl.pallas_call(
        functools.partial(finish_kernel, middle, places),
        in_specs=[SMEM] + [VMEM] * (3 + len(rights)), out_specs=VMEM,
        out_shape=jax.ShapeDtypeStruct(keep.shape, BF16),
        compiler_params=LARGE, cost_estimate=cost(2, panel, rights[0]), name="finish",
    )(where, panel, begun, *rights, keep)


def around(block, axis):
    return send(block, axis(1)), send(block, axis(3))


def opposite(up, down, axis):
    half = up.shape[0] // 2
    return send(up[:half], axis(1)), send(down[half:], axis(3))


def together(*arrays):
    return lax.optimization_barrier(arrays)


def gather(block):
    f1, f3 = around(block, first_axis)
    near = join(block, f1)
    near1, near3 = together(*around(near, second_axis))
    far = join(f3, *opposite(f1, f3, first_axis))
    near2 = opposite(near1, near3, second_axis)
    far1, far3 = together(*around(far, second_axis))
    half = block.shape[0]
    early = [near, far, near1, far1, near3, far3, *near2]
    places = [(0, 0), (1, 0), (2, 0), (3, 0), (6, 0), (7, 0), (4, 0), (4, half)]
    return early, places, opposite(far1, far3, second_axis), [(5, 0), (5, half)]


def local(matrix, pattern):
    size = matrix.shape[0]
    row, col = lax.axis_index("row"), lax.axis_index("col")
    y, x, z, c = row >> 2, row & 3, col >> 1, col & 1
    up = 1 - 2 * c
    along, against = [(z - s * up) & 7 for s in range(5)], [(z + s * up) & 7 for s in range(5)]
    tiles = [2 * a + c for a in along] + [2 * a + 1 - c for a in along[:4]]
    tiles += [2 * a + 1 - c for a in against[1:]] + [2 * a + c for a in against[1:4]]
    pairs, sides = [], []
    for tile in tiles:
        dy, dx = (y - (tile >> 2)) & 3, (x - (tile & 3)) & 3
        first, second = jnp.where(c == 0, dx, dy), jnp.where(c == 0, dy, dx)
        pairs.append(2 * second + (first >> 1))
        sides.append((first ^ (first >> 1)) & 1)
    where = jnp.stack(pairs + sides + [(row - col) * size]).astype(jnp.int32)

    matrix, where = lax.optimization_barrier((matrix, where))
    masked, keep = mask(matrix, pattern)
    own, other = [masked], [send(masked, SWAP)]
    f1, f3 = around(masked, first_axis)
    f2 = send(masked, first_axis(2))
    own.append(send(own[0], RING))
    other.append(send(other[0], RING))
    own[1], f1, f3, f2 = together(own[1], f1, f3, f2)
    full = join(masked, f1, f3, f2)
    full1, full3 = around(full, second_axis)
    for _ in range(2):
        own.append(send(own[-1], RING))
        other.append(send(other[-1], RING))
    own.append(send(own[-1], RING))
    late = opposite(full1, full3, second_axis)
    swapped = [send(a, SWAP) for a in own[1:] + other[1:]]
    swapped[-1], *late = together(swapped[-1], *late)
    panel = arrange(where, own + other + swapped)
    begun = begin(panel, [full, full1, full3], [(0, 0), (2, 0), (6, 0)])
    middle = finish(where, panel, begun, late, [(4, 0), (5, 0)], keep, True)
    early, places, late, late_places = gather(middle)
    return finish(where, panel, begin(panel, early, places), late, late_places, keep, False)


def solution(mesh):
    spec = P("row", "col")
    return jax.shard_map(local, mesh=mesh, in_specs=(spec, spec), out_specs=spec, check_vma=False)
```

```python
import functools

import jax
import jax.numpy as jnp
from jax import lax
from jax.experimental import pallas as pl
from jax.experimental.pallas import tpu as pltpu
from jax.sharding import PartitionSpec as P

BLK = 64
SIDE = 4
DEEP = 8
TILES = 16
AXES = ("row", "col")
F32 = jnp.float32
BF16 = jnp.bfloat16
VMEM = pl.BlockSpec(memory_space=pltpu.VMEM)
SMEM = pl.BlockSpec(memory_space=pltpu.SMEM)
SMALL = pltpu.CompilerParams(vmem_limit_bytes=4 << 20)
LARGE = pltpu.CompilerParams(vmem_limit_bytes=16 << 20)


def device(y, x, z, c):
    return ((y % SIDE) * SIDE + x % SIDE) * 2 * DEEP + (z % DEEP) * 2 + c


PLACES = [(y, x, z, c) for y in range(SIDE) for x in range(SIDE) for z in range(DEEP) for c in range(2)]
SWAP = [(device(y, x, z, c), device(y, x, z, 1 - c)) for y, x, z, c in PLACES]
RING = [(device(y, x, z, c), device(y, x, z + 1 - 2 * c, c)) for y, x, z, c in PLACES]


def first_axis(step):
    return [(device(y, x, z, c), device(y + step * c, x + step * (1 - c), z, c)) for y, x, z, c in PLACES]


def second_axis(step):
    return [(device(y, x, z, c), device(y + step * (1 - c), x + step * c, z, c)) for y, x, z, c in PLACES]


def send(block, pairs):
    return lax.ppermute(block, AXES, pairs)


def mask_kernel(matrix_ref, pattern_ref, out_ref, keep_ref):
    rows, cols = matrix_ref.shape
    br, bc = pattern_ref.shape
    up = (lax.broadcasted_iota(jnp.int32, (rows, br), 0) // BLK
          == lax.broadcasted_iota(jnp.int32, (rows, br), 1)).astype(F32).astype(BF16)
    across = (lax.broadcasted_iota(jnp.int32, (bc, cols), 1) // BLK
              == lax.broadcasted_iota(jnp.int32, (bc, cols), 0)).astype(F32).astype(BF16)
    pattern = pattern_ref[...].astype(F32).astype(BF16)
    tall = jnp.dot(up, pattern, preferred_element_type=F32).astype(BF16)
    keep = jnp.dot(tall, across, preferred_element_type=F32)
    keep_ref[...] = keep.astype(BF16)
    out_ref[...] = jnp.where(keep == 1.0, matrix_ref[...].astype(F32), 0.0).astype(BF16)


def mask(matrix, pattern):
    shape = jax.ShapeDtypeStruct(matrix.shape, BF16)
    return pl.pallas_call(
        mask_kernel, in_specs=[VMEM, VMEM], out_specs=[VMEM, VMEM], out_shape=[shape, shape],
        compiler_params=SMALL, name="mask",
    )(matrix, pattern)


def join_kernel(*refs):
    out_ref, first = refs[-1], 0
    for ref in refs[:-1]:
        out_ref[first:first + ref.shape[0], :] = ref[...]
        first += ref.shape[0]


def join(*parts):
    rows, cols = sum(part.shape[0] for part in parts), parts[0].shape[1]
    return pl.pallas_call(
        join_kernel, in_specs=[VMEM] * len(parts), out_specs=VMEM,
        out_shape=jax.ShapeDtypeStruct((rows, cols), BF16),
        compiler_params=SMALL, name="join",
    )(*parts)


def arrange_kernel(where_ref, *refs):
    tiles, out_ref = refs[:-1], refs[-1]
    cols = tiles[0].shape[1]
    for t, tile in enumerate(tiles):
        at = pl.multiple_of(where_ref[TILES + t] * cols, cols)
        out_ref[where_ref[t], :, pl.ds(at, cols)] = tile[...]


def arrange(where, tiles):
    rows, cols = tiles[0].shape
    return pl.pallas_call(
        arrange_kernel, in_specs=[SMEM] + [VMEM] * TILES, out_specs=VMEM,
        out_shape=jax.ShapeDtypeStruct((TILES // 2, rows, 2 * cols), BF16),
        compiler_params=SMALL, name="arrange",
    )(where, *tiles)


def cost(pairs, panel, right):
    rows, deep, cols = panel.shape[1], right.shape[0], right.shape[1]
    return pl.CostEstimate(
        flops=2 * pairs * rows * deep * cols, bytes_accessed=2 * pairs * deep * (rows + cols), transcendentals=0)


def total_of(panel_ref, rights, places):
    total = None
    for ref, (pair, first) in zip(rights, places):
        width = panel_ref.shape[2]
        for top in range(0, ref.shape[0], width):
            rows = min(width, ref.shape[0] - top)
            left = panel_ref[pair + top // width, :, first:first + rows]
            term = jnp.dot(left, ref[top:top + rows, :], preferred_element_type=F32)
            total = term if total is None else total + term
    return total


def begin_kernel(places, panel_ref, *refs):
    refs[-1][...] = total_of(panel_ref, refs[:-1], places)


def begin(panel, rights, places):
    return pl.pallas_call(
        functools.partial(begin_kernel, places), in_specs=[VMEM] * (1 + len(rights)), out_specs=VMEM,
        out_shape=jax.ShapeDtypeStruct((panel.shape[1], rights[0].shape[1]), F32),
        compiler_params=LARGE, cost_estimate=cost(0, panel, rights[0]), name="begin",
    )(panel, *rights)


def finish_kernel(middle, places, where_ref, panel_ref, sum_ref, *refs):
    keep_ref, out_ref = refs[-2:]
    total = sum_ref[...] + total_of(panel_ref, refs[:-2], places)
    total = keep_ref[...].astype(F32) * total
    if middle:
        diagonal = (lax.broadcasted_iota(jnp.int32, total.shape, 0) + where_ref[2 * TILES]
                    == lax.broadcasted_iota(jnp.int32, total.shape, 1))
        total = jnp.where(diagonal, 1.5, 0.0) - 0.5 * total
    out_ref[...] = total.astype(BF16)


def finish(where, panel, begun, rights, places, keep, middle):
    return pl.pallas_call(
        functools.partial(finish_kernel, middle, places),
        in_specs=[SMEM] + [VMEM] * (3 + len(rights)), out_specs=VMEM,
        out_shape=jax.ShapeDtypeStruct(keep.shape, BF16),
        compiler_params=LARGE, cost_estimate=cost(2, panel, rights[0]), name="finish",
    )(where, panel, begun, *rights, keep)


def around(block, axis):
    return send(block, axis(1)), send(block, axis(3))


def opposite(up, down, axis):
    half = up.shape[0] // 2
    return send(up[:half], axis(1)), send(down[half:], axis(3))


def together(*arrays):
    return lax.optimization_barrier(arrays)


def gather(block):
    f1, f3 = around(block, first_axis)
    near = join(block, f1)
    near1, near3 = together(*around(near, second_axis))
    far = join(f3, *opposite(f1, f3, first_axis))
    near2 = opposite(near1, near3, second_axis)
    far1, far3 = together(*around(far, second_axis))
    half = block.shape[0]
    early = [near, far, near1, far1, near3, far3, *near2]
    places = [(0, 0), (1, 0), (2, 0), (3, 0), (6, 0), (7, 0), (4, 0), (4, half)]
    return early, places, opposite(far1, far3, second_axis), [(5, 0), (5, half)]


def local(matrix, pattern):
    size = matrix.shape[0]
    row, col = lax.axis_index("row"), lax.axis_index("col")
    y, x, z, c = row >> 2, row & 3, col >> 1, col & 1
    up = 1 - 2 * c
    along, against = [(z - s * up) & 7 for s in range(5)], [(z + s * up) & 7 for s in range(5)]
    tiles = [2 * a + c for a in along] + [2 * a + 1 - c for a in along[:4]]
    tiles += [2 * a + 1 - c for a in against[1:]] + [2 * a + c for a in against[1:4]]
    pairs, sides = [], []
    for tile in tiles:
        dy, dx = (y - (tile >> 2)) & 3, (x - (tile & 3)) & 3
        first, second = jnp.where(c == 0, dx, dy), jnp.where(c == 0, dy, dx)
        pairs.append(2 * second + (first >> 1))
        sides.append((first ^ (first >> 1)) & 1)
    where = jnp.stack(pairs + sides + [(row - col) * size]).astype(jnp.int32)

    matrix, where = lax.optimization_barrier((matrix, where))
    masked, keep = mask(matrix, pattern)
    own, other = [masked], [send(masked, SWAP)]
    f1, f3 = around(masked, first_axis)
    f2 = send(masked, first_axis(2))
    own.append(send(own[0], RING))
    other.append(send(other[0], RING))
    own[1], other[1], f1, f3, f2 = together(own[1], other[1], f1, f3, f2)
    full = join(masked, f1, f3, f2)
    full1, full3 = around(full, second_axis)
    for _ in range(2):
        own.append(send(own[-1], RING))
        other.append(send(other[-1], RING))
    own.append(send(own[-1], RING))
    late = opposite(full1, full3, second_axis)
    swapped = [send(a, SWAP) for a in own[1:] + other[1:]]
    panel = arrange(where, own + other + swapped)
    begun = begin(panel, [full, full1, full3], [(0, 0), (2, 0), (6, 0)])
    begun, *late = together(begun, *late)
    middle = finish(where, panel, begun, late, [(4, 0), (5, 0)], keep, True)
    early, places, late, late_places = gather(middle)
    return finish(where, panel, begin(panel, early, places), late, late_places, keep, False)


def solution(mesh):
    spec = P("row", "col")
    return jax.shard_map(local, mesh=mesh, in_specs=(spec, spec), out_specs=spec, check_vma=False)
```

```python
import functools

import jax
import jax.numpy as jnp
from jax import lax
from jax.experimental import pallas as pl
from jax.experimental.pallas import tpu as pltpu
from jax.sharding import PartitionSpec as P

BLK = 64
SIDE = 4
DEEP = 8
TILES = 16
AXES = ("row", "col")
F32 = jnp.float32
BF16 = jnp.bfloat16
VMEM = pl.BlockSpec(memory_space=pltpu.VMEM)
SMEM = pl.BlockSpec(memory_space=pltpu.SMEM)
ANY = pl.BlockSpec(memory_space=pl.ANY)
SMALL = pltpu.CompilerParams(vmem_limit_bytes=4 << 20)
LARGE = pltpu.CompilerParams(vmem_limit_bytes=16 << 20)


def device(y, x, z, c):
    return ((y % SIDE) * SIDE + x % SIDE) * 2 * DEEP + (z % DEEP) * 2 + c


PLACES = [(y, x, z, c) for y in range(SIDE) for x in range(SIDE) for z in range(DEEP) for c in range(2)]
SWAP = [(device(y, x, z, c), device(y, x, z, 1 - c)) for y, x, z, c in PLACES]
RING = [(device(y, x, z, c), device(y, x, z + 1 - 2 * c, c)) for y, x, z, c in PLACES]


def first_axis(step):
    return [(device(y, x, z, c), device(y + step * c, x + step * (1 - c), z, c)) for y, x, z, c in PLACES]


def second_axis(step):
    return [(device(y, x, z, c), device(y + step * (1 - c), x + step * c, z, c)) for y, x, z, c in PLACES]


def send(block, pairs):
    return lax.ppermute(block, AXES, pairs)


def mask_kernel(matrix_ref, pattern_ref, out_ref, keep_ref):
    rows, cols = matrix_ref.shape
    br, bc = pattern_ref.shape
    up = (lax.broadcasted_iota(jnp.int32, (rows, br), 0) // BLK
          == lax.broadcasted_iota(jnp.int32, (rows, br), 1)).astype(F32).astype(BF16)
    across = (lax.broadcasted_iota(jnp.int32, (bc, cols), 1) // BLK
              == lax.broadcasted_iota(jnp.int32, (bc, cols), 0)).astype(F32).astype(BF16)
    pattern = pattern_ref[...].astype(F32).astype(BF16)
    tall = jnp.dot(up, pattern, preferred_element_type=F32).astype(BF16)
    keep = jnp.dot(tall, across, preferred_element_type=F32)
    keep_ref[...] = keep.astype(BF16)
    out_ref[...] = jnp.where(keep == 1.0, matrix_ref[...].astype(F32), 0.0).astype(BF16)


def mask(matrix, pattern):
    shape = jax.ShapeDtypeStruct(matrix.shape, BF16)
    return pl.pallas_call(
        mask_kernel, in_specs=[VMEM, VMEM], out_specs=[VMEM, VMEM], out_shape=[shape, shape],
        compiler_params=SMALL, name="mask",
    )(matrix, pattern)


def join_kernel(*refs):
    out_ref, first = refs[-1], 0
    for ref in refs[:-1]:
        out_ref[first:first + ref.shape[0], :] = ref[...]
        first += ref.shape[0]


def join(*parts):
    rows, cols = sum(part.shape[0] for part in parts), parts[0].shape[1]
    return pl.pallas_call(
        join_kernel, in_specs=[VMEM] * len(parts), out_specs=VMEM,
        out_shape=jax.ShapeDtypeStruct((rows, cols), BF16),
        compiler_params=SMALL, name="join",
    )(*parts)


def arrange_kernel(where_ref, *refs):
    tiles, out_ref = refs[:-1], refs[-1]
    cols = tiles[0].shape[1]
    for t, tile in enumerate(tiles):
        at = pl.multiple_of(where_ref[TILES + t] * cols, cols)
        out_ref[where_ref[t], :, pl.ds(at, cols)] = tile[...]


def arrange(where, tiles):
    rows, cols = tiles[0].shape
    return pl.pallas_call(
        arrange_kernel, in_specs=[SMEM] + [VMEM] * TILES, out_specs=VMEM,
        out_shape=jax.ShapeDtypeStruct((TILES // 2, rows, 2 * cols), BF16),
        compiler_params=SMALL, name="arrange",
    )(where, *tiles)


def cost(pairs, panel, right):
    rows, deep, cols = panel.shape[1], right.shape[0], right.shape[1]
    return pl.CostEstimate(
        flops=2 * pairs * rows * deep * cols, bytes_accessed=2 * pairs * deep * (rows + cols), transcendentals=0)


def total_of(panel_ref, rights, places):
    total = None
    for ref, (pair, first) in zip(rights, places):
        width = panel_ref.shape[2]
        for top in range(0, ref.shape[0], width):
            rows = min(width, ref.shape[0] - top)
            left = panel_ref[pair + top // width, :, first:first + rows]
            term = jnp.dot(left, ref[top:top + rows, :], preferred_element_type=F32)
            total = term if total is None else total + term
    return total


def begin_kernel(places, panel_ref, *refs):
    refs[-1][...] = total_of(panel_ref, refs[:-1], places)


def begin(panel, rights, places):
    return pl.pallas_call(
        functools.partial(begin_kernel, places), in_specs=[VMEM] * (1 + len(rights)), out_specs=VMEM,
        out_shape=jax.ShapeDtypeStruct((panel.shape[1], rights[0].shape[1]), F32),
        compiler_params=LARGE, cost_estimate=cost(0, panel, rights[0]), name="begin",
    )(panel, *rights)


def middle_kernel(places, where_ref, panel_ref, sum_ref, *refs):
    keep_ref, out_ref = refs[-2:]
    total = sum_ref[...] + total_of(panel_ref, refs[:-2], places)
    total = keep_ref[...].astype(F32) * total
    diagonal = (lax.broadcasted_iota(jnp.int32, total.shape, 0) + where_ref[2 * TILES]
                == lax.broadcasted_iota(jnp.int32, total.shape, 1))
    out_ref[...] = (jnp.where(diagonal, 1.5, 0.0) - 0.5 * total).astype(BF16)


def finish_middle(where, panel, begun, rights, places, keep):
    return pl.pallas_call(
        functools.partial(middle_kernel, places),
        in_specs=[SMEM] + [VMEM] * (3 + len(rights)), out_specs=VMEM,
        out_shape=jax.ShapeDtypeStruct(keep.shape, BF16),
        compiler_params=LARGE, cost_estimate=cost(2, panel, rights[0]), name="middle",
    )(where, panel, begun, *rights, keep)


def last_kernel(places, panel_ref, sum_ref, *refs):
    rights, keep_ref, out_hbm, out_ref, sems = refs[:-4], refs[-4], refs[-3], refs[-2], refs[-1]
    half = out_ref.shape[0] // 2
    stores = []
    for k in range(2):
        rows = pl.ds(k * half, half)
        total = sum_ref[rows, :] + total_of(panel_ref.at[:, rows, :], rights, places)
        out_ref[rows, :] = (keep_ref[rows, :].astype(F32) * total).astype(BF16)
        stores.append(pltpu.make_async_copy(out_ref.at[rows], out_hbm.at[rows], sems.at[k]))
        stores[-1].start()
    for store in stores:
        store.wait()


def finish_last(panel, begun, rights, places, keep):
    return pl.pallas_call(
        functools.partial(last_kernel, places),
        in_specs=[VMEM] * (3 + len(rights)), out_specs=ANY,
        out_shape=jax.ShapeDtypeStruct(keep.shape, BF16),
        scratch_shapes=[pltpu.VMEM(keep.shape, BF16), pltpu.SemaphoreType.DMA((2,))],
        compiler_params=LARGE, cost_estimate=cost(2, panel, rights[0]), name="last",
    )(panel, begun, *rights, keep)


def around(block, axis):
    return send(block, axis(1)), send(block, axis(3))


def opposite(up, down, axis):
    half = up.shape[0] // 2
    return send(up[:half], axis(1)), send(down[half:], axis(3))


def together(*arrays):
    return lax.optimization_barrier(arrays)


def gather(block):
    f1, f3 = around(block, first_axis)
    near = join(block, f1)
    near1, near3 = together(*around(near, second_axis))
    far = join(f3, *opposite(f1, f3, first_axis))
    near2 = opposite(near1, near3, second_axis)
    far1, far3 = together(*around(far, second_axis))
    half = block.shape[0]
    early = [near, far, near1, far1, near3, far3, *near2]
    places = [(0, 0), (1, 0), (2, 0), (3, 0), (6, 0), (7, 0), (4, 0), (4, half)]
    return early, places, opposite(far1, far3, second_axis), [(5, 0), (5, half)]


def local(matrix, pattern):
    size = matrix.shape[0]
    row, col = lax.axis_index("row"), lax.axis_index("col")
    y, x, z, c = row >> 2, row & 3, col >> 1, col & 1
    up = 1 - 2 * c
    along, against = [(z - s * up) & 7 for s in range(5)], [(z + s * up) & 7 for s in range(5)]
    tiles = [2 * a + c for a in along] + [2 * a + 1 - c for a in along[:4]]
    tiles += [2 * a + 1 - c for a in against[1:]] + [2 * a + c for a in against[1:4]]
    pairs, sides = [], []
    for tile in tiles:
        dy, dx = (y - (tile >> 2)) & 3, (x - (tile & 3)) & 3
        first, second = jnp.where(c == 0, dx, dy), jnp.where(c == 0, dy, dx)
        pairs.append(2 * second + (first >> 1))
        sides.append((first ^ (first >> 1)) & 1)
    where = jnp.stack(pairs + sides + [(row - col) * size]).astype(jnp.int32)

    matrix, where = lax.optimization_barrier((matrix, where))
    masked, keep = mask(matrix, pattern)
    own, other = [masked], [send(masked, SWAP)]
    f1, f3 = around(masked, first_axis)
    f2 = send(masked, first_axis(2))
    own.append(send(own[0], RING))
    other.append(send(other[0], RING))
    own[1], other[1], f1, f3, f2 = together(own[1], other[1], f1, f3, f2)
    full = join(masked, f1, f3, f2)
    full1, full3 = around(full, second_axis)
    own.append(send(own[1], RING))
    other.append(send(other[1], RING))
    own[2], own1 = together(own[2], send(own[1], SWAP))
    own.append(send(own[2], RING))
    other[2], other1 = together(other[2], send(other[1], SWAP))
    other.append(send(other[2], RING))
    own[3], own2 = together(own[3], send(own[2], SWAP))
    own.append(send(own[3], RING))
    late = opposite(full1, full3, second_axis)
    swapped = [own1, own2, send(own[3], SWAP), send(own[4], SWAP), other1, send(other[2], SWAP), send(other[3], SWAP)]
    panel = arrange(where, own + other + swapped)
    begun = begin(panel, [full, full1, full3], [(0, 0), (2, 0), (6, 0)])
    begun, *late = together(begun, *late)
    middle = finish_middle(where, panel, begun, late, [(4, 0), (5, 0)], keep)
    early, places, late, late_places = gather(middle)
    return finish_last(panel, begin(panel, early, places), late, late_places, keep)


def solution(mesh):
    spec = P("row", "col")
    return jax.shard_map(local, mesh=mesh, in_specs=(spec, spec), out_specs=spec, check_vma=False)
```

```python
import functools

import jax
import jax.numpy as jnp
from jax import lax
from jax.experimental import pallas as pl
from jax.experimental.pallas import tpu as pltpu
from jax.sharding import PartitionSpec as P

BLK = 64
SIDE = 4
DEEP = 8
TILES = 16
AXES = ("row", "col")
F32 = jnp.float32
BF16 = jnp.bfloat16
VMEM = pl.BlockSpec(memory_space=pltpu.VMEM)
SMEM = pl.BlockSpec(memory_space=pltpu.SMEM)
ANY = pl.BlockSpec(memory_space=pl.ANY)
SMALL = pltpu.CompilerParams(vmem_limit_bytes=4 << 20)
LARGE = pltpu.CompilerParams(vmem_limit_bytes=16 << 20)


def device(y, x, z, c):
    return ((y % SIDE) * SIDE + x % SIDE) * 2 * DEEP + (z % DEEP) * 2 + c


PLACES = [(y, x, z, c) for y in range(SIDE) for x in range(SIDE) for z in range(DEEP) for c in range(2)]
SWAP = [(device(y, x, z, c), device(y, x, z, 1 - c)) for y, x, z, c in PLACES]
RING = [(device(y, x, z, c), device(y, x, z + 1 - 2 * c, c)) for y, x, z, c in PLACES]


def first_axis(step):
    return [(device(y, x, z, c), device(y + step * c, x + step * (1 - c), z, c)) for y, x, z, c in PLACES]


def second_axis(step):
    return [(device(y, x, z, c), device(y + step * (1 - c), x + step * c, z, c)) for y, x, z, c in PLACES]


def send(block, pairs):
    return lax.ppermute(block, AXES, pairs)


def mask_kernel(matrix_ref, pattern_ref, out_ref, keep_ref):
    rows, cols = matrix_ref.shape
    br, bc = pattern_ref.shape
    up = (lax.broadcasted_iota(jnp.int32, (rows, br), 0) // BLK
          == lax.broadcasted_iota(jnp.int32, (rows, br), 1)).astype(F32).astype(BF16)
    across = (lax.broadcasted_iota(jnp.int32, (bc, cols), 1) // BLK
              == lax.broadcasted_iota(jnp.int32, (bc, cols), 0)).astype(F32).astype(BF16)
    pattern = pattern_ref[...].astype(F32).astype(BF16)
    tall = jnp.dot(up, pattern, preferred_element_type=F32).astype(BF16)
    keep = jnp.dot(tall, across, preferred_element_type=F32)
    keep_ref[...] = keep.astype(BF16)
    out_ref[...] = jnp.where(keep == 1.0, matrix_ref[...].astype(F32), 0.0).astype(BF16)


def mask(matrix, pattern):
    shape = jax.ShapeDtypeStruct(matrix.shape, BF16)
    return pl.pallas_call(
        mask_kernel, in_specs=[VMEM, VMEM], out_specs=[VMEM, VMEM], out_shape=[shape, shape],
        compiler_params=SMALL, name="mask",
    )(matrix, pattern)


def join_kernel(*refs):
    out_ref, first = refs[-1], 0
    for ref in refs[:-1]:
        out_ref[first:first + ref.shape[0], :] = ref[...]
        first += ref.shape[0]


def join(*parts):
    rows, cols = sum(part.shape[0] for part in parts), parts[0].shape[1]
    return pl.pallas_call(
        join_kernel, in_specs=[VMEM] * len(parts), out_specs=VMEM,
        out_shape=jax.ShapeDtypeStruct((rows, cols), BF16),
        compiler_params=SMALL, name="join",
    )(*parts)


def arrange_kernel(where_ref, *refs):
    tiles, out_ref = refs[:-1], refs[-1]
    cols = tiles[0].shape[1]
    for t, tile in enumerate(tiles):
        at = pl.multiple_of(where_ref[TILES + t] * cols, cols)
        out_ref[where_ref[t], :, pl.ds(at, cols)] = tile[...]


def arrange(where, tiles):
    rows, cols = tiles[0].shape
    return pl.pallas_call(
        arrange_kernel, in_specs=[SMEM] + [VMEM] * TILES, out_specs=VMEM,
        out_shape=jax.ShapeDtypeStruct((TILES // 2, rows, 2 * cols), BF16),
        compiler_params=SMALL, name="arrange",
    )(where, *tiles)


def cost(pairs, panel, right):
    rows, deep, cols = panel.shape[1], right.shape[0], right.shape[1]
    return pl.CostEstimate(
        flops=2 * pairs * rows * deep * cols, bytes_accessed=2 * pairs * deep * (rows + cols), transcendentals=0)


def total_of(panel_ref, rights, places):
    total = None
    for ref, (pair, first) in zip(rights, places):
        width = panel_ref.shape[2]
        for top in range(0, ref.shape[0], width):
            rows = min(width, ref.shape[0] - top)
            left = panel_ref[pair + top // width, :, first:first + rows]
            term = jnp.dot(left, ref[top:top + rows, :], preferred_element_type=F32)
            total = term if total is None else total + term
    return total


def begin_kernel(places, panel_ref, *refs):
    refs[-1][...] = total_of(panel_ref, refs[:-1], places)


def begin(panel, rights, places):
    return pl.pallas_call(
        functools.partial(begin_kernel, places), in_specs=[VMEM] * (1 + len(rights)), out_specs=VMEM,
        out_shape=jax.ShapeDtypeStruct((panel.shape[1], rights[0].shape[1]), F32),
        compiler_params=LARGE, cost_estimate=cost(0, panel, rights[0]), name="begin",
    )(panel, *rights)


def middle_kernel(places, where_ref, panel_ref, sum_ref, *refs):
    keep_ref, top_ref, low_ref = refs[-3:]
    total = sum_ref[...] + total_of(panel_ref, refs[:-3], places)
    total = keep_ref[...].astype(F32) * total
    diagonal = (lax.broadcasted_iota(jnp.int32, total.shape, 0) + where_ref[2 * TILES]
                == lax.broadcasted_iota(jnp.int32, total.shape, 1))
    out = (jnp.where(diagonal, 1.5, 0.0) - 0.5 * total).astype(BF16)
    half = top_ref.shape[0]
    top_ref[...], low_ref[...] = out[:half, :], out[half:, :]


def finish_middle(where, panel, begun, rights, places, keep):
    half = jax.ShapeDtypeStruct((keep.shape[0] // 2, keep.shape[1]), BF16)
    return pl.pallas_call(
        functools.partial(middle_kernel, places),
        in_specs=[SMEM] + [VMEM] * (3 + len(rights)), out_specs=[VMEM, VMEM],
        out_shape=[half, half],
        compiler_params=LARGE, cost_estimate=cost(2, panel, rights[0]), name="middle",
    )(where, panel, begun, *rights, keep)


def last_kernel(places, panel_ref, sum_ref, *refs):
    rights, keep_ref, out_hbm, out_ref, sems = refs[:-4], refs[-4], refs[-3], refs[-2], refs[-1]
    half = out_ref.shape[0] // 2
    stores = []
    for k in range(2):
        rows = pl.ds(k * half, half)
        total = sum_ref[rows, :] + total_of(panel_ref.at[:, rows, :], rights, places)
        out_ref[rows, :] = (keep_ref[rows, :].astype(F32) * total).astype(BF16)
        stores.append(pltpu.make_async_copy(out_ref.at[rows], out_hbm.at[rows], sems.at[k]))
        stores[-1].start()
    for store in stores:
        store.wait()


def finish_last(panel, begun, rights, places, keep):
    return pl.pallas_call(
        functools.partial(last_kernel, places),
        in_specs=[VMEM] * (3 + len(rights)), out_specs=ANY,
        out_shape=jax.ShapeDtypeStruct(keep.shape, BF16),
        scratch_shapes=[pltpu.VMEM(keep.shape, BF16), pltpu.SemaphoreType.DMA((2,))],
        compiler_params=LARGE, cost_estimate=cost(2, panel, rights[0]), name="last",
    )(panel, begun, *rights, keep)


def around(block, axis):
    return send(block, axis(1)), send(block, axis(3))


def opposite(up, down, axis):
    half = up.shape[0] // 2
    return send(up[:half], axis(1)), send(down[half:], axis(3))


def together(*arrays):
    return lax.optimization_barrier(arrays)


def gather(top, low):
    size = 2 * top.shape[0]
    f1_top, f3_low = send(top, first_axis(1)), send(low, first_axis(3))
    f1_low, f3_top = send(low, first_axis(1)), send(top, first_axis(3))
    f2_top, f2_low = send(f1_top, first_axis(1)), send(f3_low, first_axis(3))
    near = join(top, low, f1_top, f1_low)
    near1, near3 = together(*around(near, second_axis))
    far = join(f3_top, f3_low, f2_top, f2_low)
    near2 = opposite(near1, near3, second_axis)
    far1, far3 = together(*around(far, second_axis))
    early = [near, far, near1, far1, near3, far3, *near2]
    places = [(0, 0), (1, 0), (2, 0), (3, 0), (6, 0), (7, 0), (4, 0), (4, size)]
    return early, places, opposite(far1, far3, second_axis), [(5, 0), (5, size)]


def local(matrix, pattern):
    size = matrix.shape[0]
    row, col = lax.axis_index("row"), lax.axis_index("col")
    y, x, z, c = row >> 2, row & 3, col >> 1, col & 1
    up = 1 - 2 * c
    along, against = [(z - s * up) & 7 for s in range(5)], [(z + s * up) & 7 for s in range(5)]
    tiles = [2 * a + c for a in along] + [2 * a + 1 - c for a in along[:4]]
    tiles += [2 * a + 1 - c for a in against[1:]] + [2 * a + c for a in against[1:4]]
    pairs, sides = [], []
    for tile in tiles:
        dy, dx = (y - (tile >> 2)) & 3, (x - (tile & 3)) & 3
        first, second = jnp.where(c == 0, dx, dy), jnp.where(c == 0, dy, dx)
        pairs.append(2 * second + (first >> 1))
        sides.append((first ^ (first >> 1)) & 1)
    where = jnp.stack(pairs + sides + [(row - col) * size]).astype(jnp.int32)

    matrix, where = lax.optimization_barrier((matrix, where))
    masked, keep = mask(matrix, pattern)
    own, other = [masked], [send(masked, SWAP)]
    f1, f3 = around(masked, first_axis)
    f2 = send(masked, first_axis(2))
    own.append(send(own[0], RING))
    other.append(send(other[0], RING))
    own[1], other[1], f1, f3, f2 = together(own[1], other[1], f1, f3, f2)
    full = join(masked, f1, f3, f2)
    full1, full3 = around(full, second_axis)
    own.append(send(own[1], RING))
    other.append(send(other[1], RING))
    own[2], own1 = together(own[2], send(own[1], SWAP))
    own.append(send(own[2], RING))
    other[2], other1 = together(other[2], send(other[1], SWAP))
    other.append(send(other[2], RING))
    own[3], own2 = together(own[3], send(own[2], SWAP))
    own.append(send(own[3], RING))
    late = opposite(full1, full3, second_axis)
    swapped = [own1, own2, send(own[3], SWAP), send(own[4], SWAP), other1, send(other[2], SWAP), send(other[3], SWAP)]
    panel = arrange(where, own + other + swapped)
    begun = begin(panel, [full, full1, full3], [(0, 0), (2, 0), (6, 0)])
    begun, *late = together(begun, *late)
    top, low = finish_middle(where, panel, begun, late, [(4, 0), (5, 0)], keep)
    early, places, late, late_places = gather(top, low)
    return finish_last(panel, begin(panel, early, places), late, late_places, keep)


def solution(mesh):
    spec = P("row", "col")
    return jax.shard_map(local, mesh=mesh, in_specs=(spec, spec), out_specs=spec, check_vma=False)
```

```python
import functools

import jax
import jax.numpy as jnp
from jax import lax
from jax.experimental import pallas as pl
from jax.experimental.pallas import tpu as pltpu
from jax.sharding import PartitionSpec as P

BLK = 64
SIDE = 4
DEEP = 8
TILES = 16
AXES = ("row", "col")
F32 = jnp.float32
BF16 = jnp.bfloat16
VMEM = pl.BlockSpec(memory_space=pltpu.VMEM)
SMEM = pl.BlockSpec(memory_space=pltpu.SMEM)
ANY = pl.BlockSpec(memory_space=pl.ANY)
SMALL = pltpu.CompilerParams(vmem_limit_bytes=4 << 20)
LARGE = pltpu.CompilerParams(vmem_limit_bytes=16 << 20)


def device(y, x, z, c):
    return ((y % SIDE) * SIDE + x % SIDE) * 2 * DEEP + (z % DEEP) * 2 + c


PLACES = [(y, x, z, c) for y in range(SIDE) for x in range(SIDE) for z in range(DEEP) for c in range(2)]
SWAP = [(device(y, x, z, c), device(y, x, z, 1 - c)) for y, x, z, c in PLACES]
RING = [(device(y, x, z, c), device(y, x, z + 1 - 2 * c, c)) for y, x, z, c in PLACES]


def first_axis(step):
    return [(device(y, x, z, c), device(y + step * c, x + step * (1 - c), z, c)) for y, x, z, c in PLACES]


def second_axis(step):
    return [(device(y, x, z, c), device(y + step * (1 - c), x + step * c, z, c)) for y, x, z, c in PLACES]


def send(block, pairs):
    return lax.ppermute(block, AXES, pairs)


def mask_kernel(matrix_ref, pattern_ref, out_ref, keep_ref):
    rows, cols = matrix_ref.shape
    br, bc = pattern_ref.shape
    up = (lax.broadcasted_iota(jnp.int32, (rows, br), 0) // BLK
          == lax.broadcasted_iota(jnp.int32, (rows, br), 1)).astype(F32).astype(BF16)
    across = (lax.broadcasted_iota(jnp.int32, (bc, cols), 1) // BLK
              == lax.broadcasted_iota(jnp.int32, (bc, cols), 0)).astype(F32).astype(BF16)
    pattern = pattern_ref[...].astype(F32).astype(BF16)
    tall = jnp.dot(up, pattern, preferred_element_type=F32).astype(BF16)
    keep = jnp.dot(tall, across, preferred_element_type=F32)
    keep_ref[...] = keep.astype(BF16)
    out_ref[...] = jnp.where(keep == 1.0, matrix_ref[...].astype(F32), 0.0).astype(BF16)


def mask(matrix, pattern):
    shape = jax.ShapeDtypeStruct(matrix.shape, BF16)
    return pl.pallas_call(
        mask_kernel, in_specs=[VMEM, VMEM], out_specs=[VMEM, VMEM], out_shape=[shape, shape],
        compiler_params=SMALL, name="mask",
    )(matrix, pattern)


def join_kernel(*refs):
    out_ref, first = refs[-1], 0
    for ref in refs[:-1]:
        out_ref[first:first + ref.shape[0], :] = ref[...]
        first += ref.shape[0]


def join(*parts):
    rows, cols = sum(part.shape[0] for part in parts), parts[0].shape[1]
    return pl.pallas_call(
        join_kernel, in_specs=[VMEM] * len(parts), out_specs=VMEM,
        out_shape=jax.ShapeDtypeStruct((rows, cols), BF16),
        compiler_params=SMALL, name="join",
    )(*parts)


def arrange_kernel(where_ref, *refs):
    tiles, out_ref = refs[:-1], refs[-1]
    cols = tiles[0].shape[1]
    for t, tile in enumerate(tiles):
        at = pl.multiple_of(where_ref[TILES + t] * cols, cols)
        out_ref[where_ref[t], :, pl.ds(at, cols)] = tile[...]


def arrange(where, tiles):
    rows, cols = tiles[0].shape
    return pl.pallas_call(
        arrange_kernel, in_specs=[SMEM] + [VMEM] * TILES, out_specs=VMEM,
        out_shape=jax.ShapeDtypeStruct((TILES // 2, rows, 2 * cols), BF16),
        compiler_params=SMALL, name="arrange",
    )(where, *tiles)


def cost(pairs, panel, right):
    rows, deep, cols = panel.shape[1], right.shape[0], right.shape[1]
    return pl.CostEstimate(
        flops=2 * pairs * rows * deep * cols, bytes_accessed=2 * pairs * deep * (rows + cols), transcendentals=0)


def total_of(panel_ref, rights, places):
    total = None
    for ref, (pair, first) in zip(rights, places):
        width = panel_ref.shape[2]
        for top in range(0, ref.shape[0], width):
            rows = min(width, ref.shape[0] - top)
            left = panel_ref[pair + top // width, :, first:first + rows]
            term = jnp.dot(left, ref[top:top + rows, :], preferred_element_type=F32)
            total = term if total is None else total + term
    return total


def begin_kernel(places, panel_ref, *refs):
    refs[-1][...] = total_of(panel_ref, refs[:-1], places)


def begin(panel, rights, places):
    return pl.pallas_call(
        functools.partial(begin_kernel, places), in_specs=[VMEM] * (1 + len(rights)), out_specs=VMEM,
        out_shape=jax.ShapeDtypeStruct((panel.shape[1], rights[0].shape[1]), F32),
        compiler_params=LARGE, cost_estimate=cost(0, panel, rights[0]), name="begin",
    )(panel, *rights)


def more_kernel(places, panel_ref, sum_ref, *refs):
    refs[-1][...] = sum_ref[...] + total_of(panel_ref, refs[:-1], places)


def more(panel, begun, rights, places):
    return pl.pallas_call(
        functools.partial(more_kernel, places), in_specs=[VMEM] * (2 + len(rights)), out_specs=VMEM,
        out_shape=jax.ShapeDtypeStruct(begun.shape, F32),
        compiler_params=LARGE, cost_estimate=cost(0, panel, rights[0]), name="more",
    )(panel, begun, *rights)


def middle_kernel(places, where_ref, panel_ref, sum_ref, *refs):
    keep_ref, top_ref, low_ref = refs[-3:]
    total = sum_ref[...] + total_of(panel_ref, refs[:-3], places)
    total = keep_ref[...].astype(F32) * total
    diagonal = (lax.broadcasted_iota(jnp.int32, total.shape, 0) + where_ref[2 * TILES]
                == lax.broadcasted_iota(jnp.int32, total.shape, 1))
    out = (jnp.where(diagonal, 1.5, 0.0) - 0.5 * total).astype(BF16)
    half = top_ref.shape[0]
    top_ref[...], low_ref[...] = out[:half, :], out[half:, :]


def finish_middle(where, panel, begun, rights, places, keep):
    half = jax.ShapeDtypeStruct((keep.shape[0] // 2, keep.shape[1]), BF16)
    return pl.pallas_call(
        functools.partial(middle_kernel, places),
        in_specs=[SMEM] + [VMEM] * (3 + len(rights)), out_specs=[VMEM, VMEM],
        out_shape=[half, half],
        compiler_params=LARGE, cost_estimate=cost(2, panel, rights[0]), name="middle",
    )(where, panel, begun, *rights, keep)


def last_kernel(places, panel_ref, sum_ref, *refs):
    rights, keep_ref, out_hbm, out_ref, sems = refs[:-4], refs[-4], refs[-3], refs[-2], refs[-1]
    half = out_ref.shape[0] // 2
    stores = []
    for k in range(2):
        rows = pl.ds(k * half, half)
        total = sum_ref[rows, :] + total_of(panel_ref.at[:, rows, :], rights, places)
        out_ref[rows, :] = (keep_ref[rows, :].astype(F32) * total).astype(BF16)
        stores.append(pltpu.make_async_copy(out_ref.at[rows], out_hbm.at[rows], sems.at[k]))
        stores[-1].start()
    for store in stores:
        store.wait()


def finish_last(panel, begun, rights, places, keep):
    return pl.pallas_call(
        functools.partial(last_kernel, places),
        in_specs=[VMEM] * (3 + len(rights)), out_specs=ANY,
        out_shape=jax.ShapeDtypeStruct(keep.shape, BF16),
        scratch_shapes=[pltpu.VMEM(keep.shape, BF16), pltpu.SemaphoreType.DMA((2,))],
        compiler_params=LARGE, cost_estimate=cost(2, panel, rights[0]), name="last",
    )(panel, begun, *rights, keep)


def around(block, axis):
    return send(block, axis(1)), send(block, axis(3))


def opposite(up, down, axis):
    half = up.shape[0] // 2
    return send(up[:half], axis(1)), send(down[half:], axis(3))


def together(*arrays):
    return lax.optimization_barrier(arrays)


def gather(top, low):
    size = 2 * top.shape[0]
    f1_top, f3_low = send(top, first_axis(1)), send(low, first_axis(3))
    f1_low, f3_top = send(low, first_axis(1)), send(top, first_axis(3))
    f2_top, f2_low = send(f1_top, first_axis(1)), send(f3_low, first_axis(3))
    near = join(top, low, f1_top, f1_low)
    near1, near3 = together(*around(near, second_axis))
    far = join(f3_top, f3_low, f2_top, f2_low)
    near2 = opposite(near1, near3, second_axis)
    far1, far3 = together(*around(far, second_axis))
    early = [near, far, near1, far1, near3, far3, *near2]
    places = [(0, 0), (1, 0), (2, 0), (3, 0), (6, 0), (7, 0), (4, 0), (4, size)]
    return early, places, opposite(far1, far3, second_axis), [(5, 0), (5, size)]


def local(matrix, pattern):
    size = matrix.shape[0]
    row, col = lax.axis_index("row"), lax.axis_index("col")
    y, x, z, c = row >> 2, row & 3, col >> 1, col & 1
    up = 1 - 2 * c
    along, against = [(z - s * up) & 7 for s in range(5)], [(z + s * up) & 7 for s in range(5)]
    tiles = [2 * a + c for a in along] + [2 * a + 1 - c for a in along[:4]]
    tiles += [2 * a + 1 - c for a in against[1:]] + [2 * a + c for a in against[1:4]]
    pairs, sides = [], []
    for tile in tiles:
        dy, dx = (y - (tile >> 2)) & 3, (x - (tile & 3)) & 3
        first, second = jnp.where(c == 0, dx, dy), jnp.where(c == 0, dy, dx)
        pairs.append(2 * second + (first >> 1))
        sides.append((first ^ (first >> 1)) & 1)
    where = jnp.stack(pairs + sides + [(row - col) * size]).astype(jnp.int32)

    matrix, where = lax.optimization_barrier((matrix, where))
    masked, keep = mask(matrix, pattern)
    own, other = [masked], [send(masked, SWAP)]
    f1, f3 = around(masked, first_axis)
    f2 = send(masked, first_axis(2))
    own.append(send(own[0], RING))
    other.append(send(other[0], RING))
    own[1], other[1], f1, f3, f2 = together(own[1], other[1], f1, f3, f2)
    full = join(masked, f1, f3, f2)
    full1, full3 = around(full, second_axis)
    own.append(send(own[1], RING))
    other.append(send(other[1], RING))
    own[2], own1 = together(own[2], send(own[1], SWAP))
    own.append(send(own[2], RING))
    other[2], other1 = together(other[2], send(other[1], SWAP))
    other.append(send(other[2], RING))
    own[3], own2 = together(own[3], send(own[2], SWAP))
    own.append(send(own[3], RING))
    late = list(opposite(full1, full3, second_axis))
    swapped = [own1, own2, send(own[3], SWAP), send(own[4], SWAP), other1, send(other[2], SWAP), send(other[3], SWAP)]
    panel = arrange(where, own + other + swapped)
    begun = begin(panel, [full, full1, full3], [(0, 0), (2, 0), (6, 0)])
    begun, late[0] = together(begun, late[0])
    begun = more(panel, begun, late[:1], [(4, 0)])
    begun, late[1] = together(begun, late[1])
    top, low = finish_middle(where, panel, begun, late[1:], [(5, 0)], keep)
    early, places, late, late_places = gather(top, low)
    begun = more(panel, begin(panel, early, places), late[:1], late_places[:1])
    return finish_last(panel, begun, late[1:], late_places[1:], keep)


def solution(mesh):
    spec = P("row", "col")
    return jax.shard_map(local, mesh=mesh, in_specs=(spec, spec), out_specs=spec, check_vma=False)
```

```python
import functools

import jax
import jax.numpy as jnp
from jax import lax
from jax.experimental import pallas as pl
from jax.experimental.pallas import tpu as pltpu
from jax.sharding import PartitionSpec as P

BLK = 64
SIDE = 4
DEEP = 8
TILES = 16
AXES = ("row", "col")
F32 = jnp.float32
BF16 = jnp.bfloat16
VMEM = pl.BlockSpec(memory_space=pltpu.VMEM)
SMEM = pl.BlockSpec(memory_space=pltpu.SMEM)
ANY = pl.BlockSpec(memory_space=pl.ANY)
SMALL = pltpu.CompilerParams(vmem_limit_bytes=4 << 20)
LARGE = pltpu.CompilerParams(vmem_limit_bytes=16 << 20)


def device(y, x, z, c):
    return ((y % SIDE) * SIDE + x % SIDE) * 2 * DEEP + (z % DEEP) * 2 + c


PLACES = [(y, x, z, c) for y in range(SIDE) for x in range(SIDE) for z in range(DEEP) for c in range(2)]
SWAP = [(device(y, x, z, c), device(y, x, z, 1 - c)) for y, x, z, c in PLACES]
RING = [(device(y, x, z, c), device(y, x, z + 1 - 2 * c, c)) for y, x, z, c in PLACES]


def first_axis(step):
    return [(device(y, x, z, c), device(y + step * c, x + step * (1 - c), z, c)) for y, x, z, c in PLACES]


def second_axis(step):
    return [(device(y, x, z, c), device(y + step * (1 - c), x + step * c, z, c)) for y, x, z, c in PLACES]


def send(block, pairs):
    return lax.ppermute(block, AXES, pairs)


def mask_kernel(matrix_ref, pattern_ref, out_ref, keep_ref):
    rows, cols = matrix_ref.shape
    br, bc = pattern_ref.shape
    up = (lax.broadcasted_iota(jnp.int32, (rows, br), 0) // BLK
          == lax.broadcasted_iota(jnp.int32, (rows, br), 1)).astype(F32).astype(BF16)
    across = (lax.broadcasted_iota(jnp.int32, (bc, cols), 1) // BLK
              == lax.broadcasted_iota(jnp.int32, (bc, cols), 0)).astype(F32).astype(BF16)
    pattern = pattern_ref[...].astype(F32).astype(BF16)
    tall = jnp.dot(up, pattern, preferred_element_type=F32).astype(BF16)
    keep = jnp.dot(tall, across, preferred_element_type=F32)
    keep_ref[...] = keep.astype(BF16)
    out_ref[...] = jnp.where(keep == 1.0, matrix_ref[...].astype(F32), 0.0).astype(BF16)


def mask(matrix, pattern):
    shape = jax.ShapeDtypeStruct(matrix.shape, BF16)
    return pl.pallas_call(
        mask_kernel, in_specs=[VMEM, VMEM], out_specs=[VMEM, VMEM], out_shape=[shape, shape],
        compiler_params=SMALL, name="mask",
    )(matrix, pattern)


def join_kernel(*refs):
    out_ref, first = refs[-1], 0
    for ref in refs[:-1]:
        out_ref[first:first + ref.shape[0], :] = ref[...]
        first += ref.shape[0]


def join(*parts):
    rows, cols = sum(part.shape[0] for part in parts), parts[0].shape[1]
    return pl.pallas_call(
        join_kernel, in_specs=[VMEM] * len(parts), out_specs=VMEM,
        out_shape=jax.ShapeDtypeStruct((rows, cols), BF16),
        compiler_params=SMALL, name="join",
    )(*parts)


def arrange_kernel(where_ref, *refs):
    tiles, out_ref = refs[:-1], refs[-1]
    cols = tiles[0].shape[1]
    for t, tile in enumerate(tiles):
        at = pl.multiple_of(where_ref[TILES + t] * cols, cols)
        out_ref[where_ref[t], :, pl.ds(at, cols)] = tile[...]


def arrange(where, tiles):
    rows, cols = tiles[0].shape
    return pl.pallas_call(
        arrange_kernel, in_specs=[SMEM] + [VMEM] * TILES, out_specs=VMEM,
        out_shape=jax.ShapeDtypeStruct((TILES // 2, rows, 2 * cols), BF16),
        compiler_params=SMALL, name="arrange",
    )(where, *tiles)


def cost(pairs, panel, right):
    rows, deep, cols = panel.shape[1], right.shape[0], right.shape[1]
    return pl.CostEstimate(
        flops=2 * pairs * rows * deep * cols, bytes_accessed=2 * pairs * deep * (rows + cols), transcendentals=0)


def total_of(panel_ref, rights, places):
    total = None
    for ref, (pair, first) in zip(rights, places):
        width = panel_ref.shape[2]
        for top in range(0, ref.shape[0], width):
            rows = min(width, ref.shape[0] - top)
            left = panel_ref[pair + top // width, :, first:first + rows]
            term = jnp.dot(left, ref[top:top + rows, :], preferred_element_type=F32)
            total = term if total is None else total + term
    return total


def begin_kernel(places, panel_ref, *refs):
    refs[-1][...] = total_of(panel_ref, refs[:-1], places)


def begin(panel, rights, places):
    return pl.pallas_call(
        functools.partial(begin_kernel, places), in_specs=[VMEM] * (1 + len(rights)), out_specs=VMEM,
        out_shape=jax.ShapeDtypeStruct((panel.shape[1], rights[0].shape[1]), F32),
        compiler_params=LARGE, cost_estimate=cost(0, panel, rights[0]), name="begin",
    )(panel, *rights)


def more_kernel(places, panel_ref, sum_ref, *refs):
    refs[-1][...] = sum_ref[...] + total_of(panel_ref, refs[:-1], places)


def more(panel, begun, rights, places):
    return pl.pallas_call(
        functools.partial(more_kernel, places), in_specs=[VMEM] * (2 + len(rights)), out_specs=VMEM,
        out_shape=jax.ShapeDtypeStruct(begun.shape, F32),
        compiler_params=LARGE, cost_estimate=cost(0, panel, rights[0]), name="more",
    )(panel, begun, *rights)


def base_kernel(places, where_ref, panel_ref, sum_ref, keep_ref, part_ref, out_ref):
    total = keep_ref[...].astype(F32) * (sum_ref[...] + total_of(panel_ref, [part_ref], places))
    diagonal = (lax.broadcasted_iota(jnp.int32, total.shape, 0) + where_ref[2 * TILES]
                == lax.broadcasted_iota(jnp.int32, total.shape, 1))
    out_ref[...] = jnp.where(diagonal, 1.5, 0.0) - 0.5 * total


def middle_base(where, panel, begun, part, place, keep):
    return pl.pallas_call(
        functools.partial(base_kernel, [place]),
        in_specs=[SMEM] + [VMEM] * 4, out_specs=VMEM,
        out_shape=jax.ShapeDtypeStruct(begun.shape, F32),
        compiler_params=LARGE, cost_estimate=cost(0, panel, part), name="more",
    )(where, panel, begun, keep, part)


def middle_kernel(places, panel_ref, base_ref, part_ref, keep_ref, top_ref, low_ref):
    total = total_of(panel_ref, [part_ref], places)
    out = (base_ref[...] - 0.5 * (keep_ref[...].astype(F32) * total)).astype(BF16)
    half = top_ref.shape[0]
    top_ref[...], low_ref[...] = out[:half, :], out[half:, :]


def finish_middle(panel, base, part, place, keep):
    half = jax.ShapeDtypeStruct((keep.shape[0] // 2, keep.shape[1]), BF16)
    return pl.pallas_call(
        functools.partial(middle_kernel, [place]),
        in_specs=[VMEM] * 4, out_specs=[VMEM, VMEM],
        out_shape=[half, half],
        compiler_params=LARGE, cost_estimate=cost(2, panel, part), name="middle",
    )(panel, base, part, keep)


def last_kernel(places, panel_ref, sum_ref, *refs):
    rights, keep_ref, out_hbm, out_ref, sems = refs[:-4], refs[-4], refs[-3], refs[-2], refs[-1]
    half = out_ref.shape[0] // 2
    stores = []
    for k in range(2):
        rows = pl.ds(k * half, half)
        total = sum_ref[rows, :] + total_of(panel_ref.at[:, rows, :], rights, places)
        out_ref[rows, :] = (keep_ref[rows, :].astype(F32) * total).astype(BF16)
        stores.append(pltpu.make_async_copy(out_ref.at[rows], out_hbm.at[rows], sems.at[k]))
        stores[-1].start()
    for store in stores:
        store.wait()


def finish_last(panel, begun, rights, places, keep):
    return pl.pallas_call(
        functools.partial(last_kernel, places),
        in_specs=[VMEM] * (3 + len(rights)), out_specs=ANY,
        out_shape=jax.ShapeDtypeStruct(keep.shape, BF16),
        scratch_shapes=[pltpu.VMEM(keep.shape, BF16), pltpu.SemaphoreType.DMA((2,))],
        compiler_params=LARGE, cost_estimate=cost(2, panel, rights[0]), name="last",
    )(panel, begun, *rights, keep)


def around(block, axis):
    return send(block, axis(1)), send(block, axis(3))


def opposite(up, down, axis):
    half = up.shape[0] // 2
    return send(up[:half], axis(1)), send(down[half:], axis(3))


def together(*arrays):
    return lax.optimization_barrier(arrays)


def gather(top, low):
    size = 2 * top.shape[0]
    f1_top, f3_low = send(top, first_axis(1)), send(low, first_axis(3))
    f1_low, f3_top = send(low, first_axis(1)), send(top, first_axis(3))
    f2_top, f2_low = send(f1_top, first_axis(1)), send(f3_low, first_axis(3))
    near = join(top, low, f1_top, f1_low)
    near1, near3 = together(*around(near, second_axis))
    far = join(f3_top, f3_low, f2_top, f2_low)
    near2 = opposite(near1, near3, second_axis)
    far1, far3 = together(*around(far, second_axis))
    early = [near, far, near1, far1, near3, far3, *near2]
    places = [(0, 0), (1, 0), (2, 0), (3, 0), (6, 0), (7, 0), (4, 0), (4, size)]
    return early, places, opposite(far1, far3, second_axis), [(5, 0), (5, size)]


def local(matrix, pattern):
    size = matrix.shape[0]
    row, col = lax.axis_index("row"), lax.axis_index("col")
    y, x, z, c = row >> 2, row & 3, col >> 1, col & 1
    up = 1 - 2 * c
    along, against = [(z - s * up) & 7 for s in range(5)], [(z + s * up) & 7 for s in range(5)]
    tiles = [2 * a + c for a in along] + [2 * a + 1 - c for a in along[:4]]
    tiles += [2 * a + 1 - c for a in against[1:]] + [2 * a + c for a in against[1:4]]
    pairs, sides = [], []
    for tile in tiles:
        dy, dx = (y - (tile >> 2)) & 3, (x - (tile & 3)) & 3
        first, second = jnp.where(c == 0, dx, dy), jnp.where(c == 0, dy, dx)
        pairs.append(2 * second + (first >> 1))
        sides.append((first ^ (first >> 1)) & 1)
    where = jnp.stack(pairs + sides + [(row - col) * size]).astype(jnp.int32)

    matrix, where = lax.optimization_barrier((matrix, where))
    masked, keep = mask(matrix, pattern)
    own, other = [masked], [send(masked, SWAP)]
    f1, f3 = around(masked, first_axis)
    f2 = send(masked, first_axis(2))
    own.append(send(own[0], RING))
    other.append(send(other[0], RING))
    own[1], other[1], f1, f3, f2 = together(own[1], other[1], f1, f3, f2)
    full = join(masked, f1, f3, f2)
    full1, full3 = around(full, second_axis)
    own.append(send(own[1], RING))
    other.append(send(other[1], RING))
    own[2], own1 = together(own[2], send(own[1], SWAP))
    own.append(send(own[2], RING))
    other[2], other1 = together(other[2], send(other[1], SWAP))
    other.append(send(other[2], RING))
    own[3], own2 = together(own[3], send(own[2], SWAP))
    own.append(send(own[3], RING))
    late = list(opposite(full1, full3, second_axis))
    swapped = [own1, own2, send(own[3], SWAP), send(own[4], SWAP), other1, send(other[2], SWAP), send(other[3], SWAP)]
    panel = arrange(where, own + other + swapped)
    begun = begin(panel, [full, full1, full3], [(0, 0), (2, 0), (6, 0)])
    begun, late[0] = together(begun, late[0])
    base = middle_base(where, panel, begun, late[0], (4, 0), keep)
    base, late[1] = together(base, late[1])
    top, low = finish_middle(panel, base, late[1], (5, 0), keep)
    early, places, late, late_places = gather(top, low)
    begun = more(panel, begin(panel, early, places), late[:1], late_places[:1])
    return finish_last(panel, begun, late[1:], late_places[1:], keep)


def solution(mesh):
    spec = P("row", "col")
    return jax.shard_map(local, mesh=mesh, in_specs=(spec, spec), out_specs=spec, check_vma=False)
```

```python
import functools

import jax
import jax.numpy as jnp
from jax import lax
from jax.experimental import pallas as pl
from jax.experimental.pallas import tpu as pltpu
from jax.sharding import PartitionSpec as P

BLK = 64
SIDE = 4
DEEP = 8
TILES = 16
STORES = 4
AXES = ("row", "col")
F32 = jnp.float32
BF16 = jnp.bfloat16
VMEM = pl.BlockSpec(memory_space=pltpu.VMEM)
SMEM = pl.BlockSpec(memory_space=pltpu.SMEM)
ANY = pl.BlockSpec(memory_space=pl.ANY)
SMALL = pltpu.CompilerParams(vmem_limit_bytes=4 << 20)
LARGE = pltpu.CompilerParams(vmem_limit_bytes=16 << 20)


def device(y, x, z, c):
    return ((y % SIDE) * SIDE + x % SIDE) * 2 * DEEP + (z % DEEP) * 2 + c


PLACES = [(y, x, z, c) for y in range(SIDE) for x in range(SIDE) for z in range(DEEP) for c in range(2)]
SWAP = [(device(y, x, z, c), device(y, x, z, 1 - c)) for y, x, z, c in PLACES]
RING = [(device(y, x, z, c), device(y, x, z + 1 - 2 * c, c)) for y, x, z, c in PLACES]


def first_axis(step):
    return [(device(y, x, z, c), device(y + step * c, x + step * (1 - c), z, c)) for y, x, z, c in PLACES]


def second_axis(step):
    return [(device(y, x, z, c), device(y + step * (1 - c), x + step * c, z, c)) for y, x, z, c in PLACES]


def send(block, pairs):
    return lax.ppermute(block, AXES, pairs)


def mask_kernel(matrix_ref, pattern_ref, out_ref, keep_ref):
    rows, cols = matrix_ref.shape
    br, bc = pattern_ref.shape
    up = (lax.broadcasted_iota(jnp.int32, (rows, br), 0) // BLK
          == lax.broadcasted_iota(jnp.int32, (rows, br), 1)).astype(F32).astype(BF16)
    across = (lax.broadcasted_iota(jnp.int32, (bc, cols), 1) // BLK
              == lax.broadcasted_iota(jnp.int32, (bc, cols), 0)).astype(F32).astype(BF16)
    pattern = pattern_ref[...].astype(F32).astype(BF16)
    tall = jnp.dot(up, pattern, preferred_element_type=F32).astype(BF16)
    keep = jnp.dot(tall, across, preferred_element_type=F32)
    keep_ref[...] = keep.astype(BF16)
    out_ref[...] = jnp.where(keep == 1.0, matrix_ref[...].astype(F32), 0.0).astype(BF16)


def mask(matrix, pattern):
    shape = jax.ShapeDtypeStruct(matrix.shape, BF16)
    return pl.pallas_call(
        mask_kernel, in_specs=[VMEM, VMEM], out_specs=[VMEM, VMEM], out_shape=[shape, shape],
        compiler_params=SMALL, name="mask",
    )(matrix, pattern)


def join_kernel(*refs):
    out_ref, first = refs[-1], 0
    for ref in refs[:-1]:
        out_ref[first:first + ref.shape[0], :] = ref[...]
        first += ref.shape[0]


def join(*parts):
    rows, cols = sum(part.shape[0] for part in parts), parts[0].shape[1]
    return pl.pallas_call(
        join_kernel, in_specs=[VMEM] * len(parts), out_specs=VMEM,
        out_shape=jax.ShapeDtypeStruct((rows, cols), BF16),
        compiler_params=SMALL, name="join",
    )(*parts)


def arrange_kernel(where_ref, *refs):
    tiles, out_ref = refs[:-1], refs[-1]
    cols = tiles[0].shape[1]
    for t, tile in enumerate(tiles):
        at = pl.multiple_of(where_ref[TILES + t] * cols, cols)
        out_ref[where_ref[t], :, pl.ds(at, cols)] = tile[...]


def arrange(where, tiles):
    rows, cols = tiles[0].shape
    return pl.pallas_call(
        arrange_kernel, in_specs=[SMEM] + [VMEM] * TILES, out_specs=VMEM,
        out_shape=jax.ShapeDtypeStruct((TILES // 2, rows, 2 * cols), BF16),
        compiler_params=SMALL, name="arrange",
    )(where, *tiles)


def cost(pairs, panel, right):
    rows, deep, cols = panel.shape[1], right.shape[0], right.shape[1]
    return pl.CostEstimate(
        flops=2 * pairs * rows * deep * cols, bytes_accessed=2 * pairs * deep * (rows + cols), transcendentals=0)


def total_of(panel_ref, rights, places):
    total = None
    for ref, (pair, first) in zip(rights, places):
        width = panel_ref.shape[2]
        for top in range(0, ref.shape[0], width):
            rows = min(width, ref.shape[0] - top)
            left = panel_ref[pair + top // width, :, first:first + rows]
            term = jnp.dot(left, ref[top:top + rows, :], preferred_element_type=F32)
            total = term if total is None else total + term
    return total


def begin_kernel(places, panel_ref, *refs):
    refs[-1][...] = total_of(panel_ref, refs[:-1], places)


def begin(panel, rights, places):
    return pl.pallas_call(
        functools.partial(begin_kernel, places), in_specs=[VMEM] * (1 + len(rights)), out_specs=VMEM,
        out_shape=jax.ShapeDtypeStruct((panel.shape[1], rights[0].shape[1]), F32),
        compiler_params=LARGE, cost_estimate=cost(0, panel, rights[0]), name="begin",
    )(panel, *rights)


def more_kernel(places, panel_ref, sum_ref, *refs):
    refs[-1][...] = sum_ref[...] + total_of(panel_ref, refs[:-1], places)


def more(panel, begun, rights, places):
    return pl.pallas_call(
        functools.partial(more_kernel, places), in_specs=[VMEM] * (2 + len(rights)), out_specs=VMEM,
        out_shape=jax.ShapeDtypeStruct(begun.shape, F32),
        compiler_params=LARGE, cost_estimate=cost(0, panel, rights[0]), name="more",
    )(panel, begun, *rights)


def base_kernel(places, where_ref, panel_ref, sum_ref, keep_ref, part_ref, out_ref):
    total = keep_ref[...].astype(F32) * (sum_ref[...] + total_of(panel_ref, [part_ref], places))
    diagonal = (lax.broadcasted_iota(jnp.int32, total.shape, 0) + where_ref[2 * TILES]
                == lax.broadcasted_iota(jnp.int32, total.shape, 1))
    out_ref[...] = jnp.where(diagonal, 1.5, 0.0) - 0.5 * total


def middle_base(where, panel, begun, part, place, keep):
    return pl.pallas_call(
        functools.partial(base_kernel, [place]),
        in_specs=[SMEM] + [VMEM] * 4, out_specs=VMEM,
        out_shape=jax.ShapeDtypeStruct(begun.shape, F32),
        compiler_params=LARGE, cost_estimate=cost(0, panel, part), name="more",
    )(where, panel, begun, keep, part)


def middle_kernel(places, panel_ref, base_ref, part_ref, keep_ref, top_ref, low_ref):
    total = total_of(panel_ref, [part_ref], places)
    out = (base_ref[...] - 0.5 * (keep_ref[...].astype(F32) * total)).astype(BF16)
    half = top_ref.shape[0]
    top_ref[...], low_ref[...] = out[:half, :], out[half:, :]


def finish_middle(panel, base, part, place, keep):
    half = jax.ShapeDtypeStruct((keep.shape[0] // 2, keep.shape[1]), BF16)
    return pl.pallas_call(
        functools.partial(middle_kernel, [place]),
        in_specs=[VMEM] * 4, out_specs=[VMEM, VMEM],
        out_shape=[half, half],
        compiler_params=LARGE, cost_estimate=cost(2, panel, part), name="middle",
    )(panel, base, part, keep)


def last_kernel(places, panel_ref, sum_ref, *refs):
    rights, keep_ref, out_hbm, out_ref, sems = refs[:-4], refs[-4], refs[-3], refs[-2], refs[-1]
    part = out_ref.shape[0] // STORES
    stores = []
    for k in range(STORES):
        rows = pl.ds(k * part, part)
        total = sum_ref[rows, :] + total_of(panel_ref.at[:, rows, :], rights, places)
        out_ref[rows, :] = (keep_ref[rows, :].astype(F32) * total).astype(BF16)
        stores.append(pltpu.make_async_copy(out_ref.at[rows], out_hbm.at[rows], sems.at[k]))
        stores[-1].start()
    for store in stores:
        store.wait()


def finish_last(panel, begun, rights, places, keep):
    return pl.pallas_call(
        functools.partial(last_kernel, places),
        in_specs=[VMEM] * (3 + len(rights)), out_specs=ANY,
        out_shape=jax.ShapeDtypeStruct(keep.shape, BF16),
        scratch_shapes=[pltpu.VMEM(keep.shape, BF16), pltpu.SemaphoreType.DMA((STORES,))],
        compiler_params=LARGE, cost_estimate=cost(2, panel, rights[0]), name="last",
    )(panel, begun, *rights, keep)


def around(block, axis):
    return send(block, axis(1)), send(block, axis(3))


def opposite(up, down, axis):
    half = up.shape[0] // 2
    return send(up[:half], axis(1)), send(down[half:], axis(3))


def together(*arrays):
    return lax.optimization_barrier(arrays)


def gather(top, low):
    size = 2 * top.shape[0]
    f1_top, f3_low = send(top, first_axis(1)), send(low, first_axis(3))
    f1_low, f3_top = send(low, first_axis(1)), send(top, first_axis(3))
    f2_top, f2_low = send(f1_top, first_axis(1)), send(f3_low, first_axis(3))
    near = join(top, low, f1_top, f1_low)
    near1, near3 = together(*around(near, second_axis))
    far = join(f3_top, f3_low, f2_top, f2_low)
    near2 = opposite(near1, near3, second_axis)
    far1, far3 = together(*around(far, second_axis))
    early = [near, far, near1, far1, near3, far3, *near2]
    places = [(0, 0), (1, 0), (2, 0), (3, 0), (6, 0), (7, 0), (4, 0), (4, size)]
    return early, places, opposite(far1, far3, second_axis), [(5, 0), (5, size)]


def local(matrix, pattern):
    size = matrix.shape[0]
    row, col = lax.axis_index("row"), lax.axis_index("col")
    y, x, z, c = row >> 2, row & 3, col >> 1, col & 1
    up = 1 - 2 * c
    along, against = [(z - s * up) & 7 for s in range(5)], [(z + s * up) & 7 for s in range(5)]
    tiles = [2 * a + c for a in along] + [2 * a + 1 - c for a in along[:4]]
    tiles += [2 * a + 1 - c for a in against[1:]] + [2 * a + c for a in against[1:4]]
    pairs, sides = [], []
    for tile in tiles:
        dy, dx = (y - (tile >> 2)) & 3, (x - (tile & 3)) & 3
        first, second = jnp.where(c == 0, dx, dy), jnp.where(c == 0, dy, dx)
        pairs.append(2 * second + (first >> 1))
        sides.append((first ^ (first >> 1)) & 1)
    where = jnp.stack(pairs + sides + [(row - col) * size]).astype(jnp.int32)

    matrix, where = lax.optimization_barrier((matrix, where))
    masked, keep = mask(matrix, pattern)
    own, other = [masked], [send(masked, SWAP)]
    f1, f3 = around(masked, first_axis)
    f2 = send(masked, first_axis(2))
    own.append(send(own[0], RING))
    other.append(send(other[0], RING))
    own[1], other[1], f1, f3, f2 = together(own[1], other[1], f1, f3, f2)
    full = join(masked, f1, f3, f2)
    full1, full3 = around(full, second_axis)
    own.append(send(own[1], RING))
    other.append(send(other[1], RING))
    own[2], own1 = together(own[2], send(own[1], SWAP))
    own.append(send(own[2], RING))
    other[2], other1 = together(other[2], send(other[1], SWAP))
    other.append(send(other[2], RING))
    own[3], own2 = together(own[3], send(own[2], SWAP))
    own.append(send(own[3], RING))
    late = list(opposite(full1, full3, second_axis))
    swapped = [own1, own2, send(own[3], SWAP), send(own[4], SWAP), other1, send(other[2], SWAP), send(other[3], SWAP)]
    panel = arrange(where, own + other + swapped)
    begun = begin(panel, [full, full1, full3], [(0, 0), (2, 0), (6, 0)])
    begun, late[0] = together(begun, late[0])
    base = middle_base(where, panel, begun, late[0], (4, 0), keep)
    base, late[1] = together(base, late[1])
    top, low = finish_middle(panel, base, late[1], (5, 0), keep)
    early, places, late, late_places = gather(top, low)
    begun = more(panel, begin(panel, early, places), late[:1], late_places[:1])
    return finish_last(panel, begun, late[1:], late_places[1:], keep)


def solution(mesh):
    spec = P("row", "col")
    return jax.shard_map(local, mesh=mesh, in_specs=(spec, spec), out_specs=spec, check_vma=False)
```
